256 devices in a mesh: clip: 4 (over z_lo), seq: 16 (over x, y), expert: 4 (over z_hi, core).
Axes of the slice: x: 4, y: 4, z: 8 (z_hi: 2, z_lo: 4; z = z_hi * 4 + z_lo), core: 2. Of those that a mesh axis runs over, the one named last changes fastest.
Arguments:
- tokens: bfloat16 [262144, 1024], P(('clip', 'seq'), 'expert'), parts along dimension 0, may hold values from -55 to 55
- slot_keys: bfloat16 [1024, 32], P('expert'), may hold values from -0.390625 to 0.390625
- w_in: bfloat16 [32, 1024, 4096], P('expert', None, 'seq'), may hold values from -1.5 to 1.5
- w_out: bfloat16 [32, 4096, 1024], P('expert', 'seq'), may hold values from -0.09375 to 0.09375
Outputs:
- mixed_out: float32 [262144, 1024], P(('clip', 'seq'), 'expert'), parts along dimension 0
The draws below stay inside these ranges and needn't reach their ends.
There are 4 independent parts, one for each index of `clip`. The reference program is written for one: setup_inputs(seed, part) draws one part's arguments, and reference() takes and returns one part's arrays. A program takes and returns all parts, laid end to end along the dimension named above; an argument that names none is the same for every part. Nothing has to cross between parts.
All inputs are finite; a program needn't handle non-finite values.
Results may differ from the reference program's by a relative error of at most 0.015.
Values may be sent and summed in bfloat16 or wider, within the bound.
No kernel may reach another device: no remote copies, remote signals or barrier semaphores. Data moves between devices by JAX's collectives and lax.ppermute only.
A program may use at most 64 MiB of HBM per device.

```python
import jax
import jax.numpy as jnp
from jax import lax

D = 1024
FF = 4096
EXPERTS = 32
TOKENS = 65536


def draw_tokens(key, part):
    key = jax.random.fold_in(key, 11)
    base_key = jax.random.fold_in(key, 0)
    values = jnp.clip(jax.random.normal(base_key, (TOKENS, D), jnp.float32), -5.0, 5.0)
    return values.astype(jnp.bfloat16)


def block_scale(key, extent, pieces, least, top_value):
    def one(position, shards_of):
        draws = jax.random.uniform(jax.random.fold_in(jax.random.fold_in(key, 6), position), (shards_of,), jnp.float32, least / len(pieces), top_value / len(pieces))
        return jnp.repeat(jnp.exp(draws), extent[position] // shards_of).reshape((-1,) + (1,) * (len(extent) - position - 1))

    gain = one(*pieces[0])
    for cut in pieces[1:]:
        gain = gain * one(*cut)
    return gain


def gaussian(rng, dims, scale, reach, cuts=(), held_as=jnp.bfloat16):
    drawn = jax.random.normal(rng, dims, jnp.float32) * scale
    if len(cuts) > 0:
        drawn = block_scale(rng, dims, cuts, -0.22, 0.18) * drawn
    return jnp.clip(drawn, min=-reach, max=reach).astype(held_as)


def setup_inputs(seed: int = 0, part: int = 0) -> dict:
    seeds = jax.random.split(jax.random.key(seed), 5)
    own_keys = jax.random.split(jax.random.fold_in(seeds[4], part), 5)
    return {
        "tokens": draw_tokens(jax.random.fold_in(jax.random.fold_in(seeds[4], part), 71), part),
        "slot_keys": gaussian(seeds[1], (D, EXPERTS), (2.5 / D ** 0.5), 0.390625, ((0, 4),)),
        "w_in": gaussian(seeds[2], (EXPERTS, D, FF), 16 ** -0.5, 1.5, ((0, 4), (2, 16))),
        "w_out": gaussian(seeds[3], (EXPERTS, FF, D), FF ** -0.5, 0.09375, ((0, 4), (1, 16))),
    }


def expert_row(entries):
    slot_row, first_proj, second_proj = entries
    inner = jnp.dot(slot_row[None, :], first_proj, preferred_element_type=jnp.float32)
    hidden = jax.nn.gelu(inner, approximate=False).astype(jnp.bfloat16)
    return jnp.dot(hidden, second_proj, preferred_element_type=jnp.float32)[0]


def reference(tokens, slot_keys, w_in, w_out):
    logits = jnp.dot(tokens, slot_keys, preferred_element_type=jnp.float32)
    top_slot = jnp.max(logits, axis=0)
    dispatch = jnp.exp(logits - top_slot[None, :]).astype(jnp.bfloat16)
    totals = jnp.sum(dispatch.astype(jnp.float32), axis=0)
    gathered = jnp.dot(dispatch.T, tokens, preferred_element_type=jnp.float32)
    slot_in = (gathered / totals[:, None]).astype(jnp.bfloat16)
    slot_out = lax.map(expert_row, (slot_in, w_in, w_out))
    combine = jax.nn.softmax(logits, axis=1).astype(jnp.bfloat16)
    mixed_out = jnp.dot(combine.astype(jnp.float32), slot_out, preferred_element_type=jnp.float32)
    return mixed_out
```

```python
import jax
import jax.numpy as jnp
from jax import lax
from jax.sharding import PartitionSpec as P

BF16 = jnp.bfloat16
F32 = jnp.float32


def swap(value, z_step, core_step):
    pairs = [
        (z * 2 + c, (z ^ z_step) * 2 + (c ^ core_step)) for z in range(2) for c in range(2)
    ]
    return lax.ppermute(value, "expert", pairs)


def full_logits(tokens, slot_keys):
    count = tokens.shape[0]
    half = count // 2
    core = lax.axis_index("expert") % 2
    partial = lax.dot_general(
        slot_keys, tokens, (((0,), (1,)), ((), ())), preferred_element_type=F32
    )
    theirs = jnp.where(core == 0, partial[:, half:], partial[:, :half])
    mine = jnp.where(core == 0, partial[:, :half], partial[:, half:])
    mine = mine + swap(theirs, 0, 1)
    mine = mine + swap(mine, 1, 0)
    other = swap(mine, 0, 1)
    return jnp.concatenate(
        [jnp.where(core == 0, mine, other), jnp.where(core == 0, other, mine)], axis=1
    )


def spread(value):
    first = lax.reduce_precision(value, 8, 7)
    second = lax.reduce_precision(value - first, 8, 7)
    third = value - first - second
    return jnp.stack([first, second, third], axis=-1).astype(BF16)


def local(tokens, slot_keys, w_in, w_out):
    seq = lax.axis_size("seq")
    expert = lax.axis_size("expert")
    group = ("seq", "expert")
    slots = slot_keys.shape[1]
    width = tokens.shape[1]
    own = slots // expert

    logits = full_logits(tokens, slot_keys)
    top = jnp.max(logits, axis=1)
    dispatch = jnp.exp(logits - top[:, None]).astype(BF16)
    combine = jax.nn.softmax(logits, axis=0).astype(BF16)
    totals = jnp.sum(dispatch.astype(F32), axis=1)
    weighted = jnp.dot(dispatch, tokens, preferred_element_type=F32)
    mean = (weighted / totals[:, None]).astype(BF16)
    weight = spread(top + jnp.log(totals))
    weight = jnp.pad(weight, ((0, 0), (0, 125)))
    send = jnp.concatenate([mean, weight], axis=1).reshape(1, expert, own, width + 128)
    send = jnp.broadcast_to(send, (seq, expert, own, width + 128))
    got = lax.all_to_all(send.reshape(seq * expert, own, width + 128), group, 0, 0)
    got = got.reshape(seq, expert, own, width + 128).astype(F32)
    weight = jnp.sum(got[..., width : width + 3], axis=-1, keepdims=True)
    scale = jax.nn.softmax(weight, axis=0)
    slot_in = jnp.sum(got[..., :width] * scale, axis=0).astype(BF16)
    slot_in = slot_in.transpose(1, 0, 2).reshape(own, expert * width)

    inner = jnp.einsum("ed,edf->ef", slot_in, w_in, preferred_element_type=F32)
    hidden = jax.nn.gelu(inner, approximate=False).astype(BF16)
    partial_out = jnp.einsum("ef,efd->ed", hidden, w_out, preferred_element_type=F32)
    back = partial_out.astype(BF16).reshape(own, expert, width).transpose(1, 0, 2)
    back = jnp.broadcast_to(back[None], (seq, expert, own, width))
    back = lax.all_to_all(back.reshape(seq * expert, own, width), group, 0, 0)
    back = back.reshape(seq, slots, width).astype(F32)
    returned = jnp.sum(back, axis=0).astype(BF16)
    return lax.dot_general(
        combine, returned, (((0,), (0,)), ((), ())), preferred_element_type=F32
    )


def solution(mesh):
    return jax.shard_map(
        local,
        mesh=mesh,
        in_specs=(
            P(("clip", "seq"), "expert"),
            P("expert", None),
            P("expert", None, "seq"),
            P("expert", "seq", None),
        ),
        out_specs=P(("clip", "seq"), "expert"),
        check_vma=False,
    )
```

```python
import jax
import jax.numpy as jnp
from jax import lax
from jax.experimental import pallas as pl
from jax.experimental.pallas import tpu as pltpu
from jax.sharding import PartitionSpec as P

BF16 = jnp.bfloat16
F32 = jnp.float32
LANES = 128
REACH = 125.0
BLOCK = 512


def swap(value, z_step, core_step):
    pairs = [
        (z * 2 + c, (z ^ z_step) * 2 + (c ^ core_step)) for z in range(2) for c in range(2)
    ]
    return lax.ppermute(value, "expert", pairs)


def spread(value):
    first = lax.reduce_precision(value, 8, 7)
    second = lax.reduce_precision(value - first, 8, 7)
    return [first, second, value - first - second]


def exchanged(scores):
    high = jnp.max(scores, axis=1)
    low = jnp.min(scores, axis=1)
    center = 0.5 * (high + low)
    span = jnp.maximum(high - low, 1e-30)
    code = jnp.exp2((scores - center[:, None]) * (2 * REACH / span)[:, None])
    side = jnp.stack(spread(center) + spread(span), axis=1)
    side = jnp.pad(side, ((0, 0), (0, LANES - side.shape[1])))
    sent = jnp.concatenate([code, side], axis=1).astype(BF16)
    got = swap(sent, 1, 0).astype(F32)
    count = scores.shape[1]
    center = jnp.sum(got[:, count : count + 3], axis=1, keepdims=True)
    span = jnp.sum(got[:, count + 3 : count + 6], axis=1, keepdims=True)
    return jnp.log2(got[:, :count]) * (span / (2 * REACH)) + center


def full_logits(tokens, slot_keys):
    count = tokens.shape[0]
    half = count // 2
    core = lax.axis_index("expert") % 2
    partial = lax.dot_general(
        slot_keys, tokens, (((0,), (1,)), ((), ())), preferred_element_type=F32
    )
    theirs = jnp.where(core == 0, partial[:, half:], partial[:, :half])
    mine = jnp.where(core == 0, partial[:, :half], partial[:, half:])
    mine = mine + swap(theirs, 0, 1)
    mine = mine + exchanged(mine)
    other = swap(mine, 0, 1)
    return jnp.concatenate(
        [jnp.where(core == 0, mine, other), jnp.where(core == 0, other, mine)], axis=1
    )


def experts(got, w_in, w_out, seq, expert):
    own, width = w_in.shape[0], w_in.shape[1] // expert
    hidden_width = w_in.shape[2]

    def kernel(got_ref, w_in_ref, w_out_ref, out_ref):
        weight = jnp.sum(got_ref[:, :, width:].astype(F32), axis=-1, keepdims=True)
        weight = weight.reshape(seq, expert, own, 1)
        scale = jnp.exp(weight - jnp.max(weight, axis=0, keepdims=True))
        scale = scale / jnp.sum(scale, axis=0, keepdims=True)
        pieces = []
        for e in range(expert):
            total = jnp.zeros((own, width), F32)
            for s in range(seq):
                total += got_ref[s * expert + e, :, :width].astype(F32) * scale[s, e]
            pieces.append(total.astype(BF16))
        rows = lax.broadcasted_iota(jnp.int32, (own, hidden_width), 0)
        inner = jnp.zeros((own, hidden_width), F32)
        for i in range(own):
            total = jnp.zeros((own, hidden_width), F32)
            for e in range(expert):
                total += jnp.dot(
                    pieces[e],
                    w_in_ref[i, e * width : (e + 1) * width, :],
                    preferred_element_type=F32,
                )
            inner = jnp.where(rows == i, total, inner)
        hidden = 0.5 * inner * (1.0 + lax.erf(inner * (0.5**0.5)))
        hidden = hidden.astype(BF16)
        for e in range(expert):
            rows = lax.broadcasted_iota(jnp.int32, (own, width), 0)
            result = jnp.zeros((own, width), F32)
            for i in range(own):
                part = jnp.dot(
                    hidden,
                    w_out_ref[i, :, e * width : (e + 1) * width],
                    preferred_element_type=F32,
                )
                result = jnp.where(rows == i, part, result)
            result = result.astype(BF16)
            for s in range(seq):
                out_ref[s * expert + e] = result

    whole = pl.BlockSpec(memory_space=pltpu.VMEM)
    return pl.pallas_call(
        kernel,
        out_shape=jax.ShapeDtypeStruct((seq * expert, own, width), BF16),
        in_specs=[whole, whole, whole],
        out_specs=whole,
        compiler_params=pltpu.CompilerParams(vmem_limit_bytes=24 * 2**20),
        cost_estimate=pl.CostEstimate(
            flops=4 * own * width * expert * hidden_width * own,
            bytes_accessed=2 * (w_in.size + w_out.size),
            transcendentals=own * hidden_width,
        ),
        name="experts",
    )(
        got,
        pltpu.with_memory_space_constraint(w_in, pltpu.VMEM),
        pltpu.with_memory_space_constraint(w_out, pltpu.VMEM),
    )


def mix(combine, back, seq, expert):
    slots, count = combine.shape
    width = back.shape[2]
    own = slots // expert

    def kernel(combine_ref, back_ref, out_ref, table):
        @pl.when(pl.program_id(0) == 0)
        def _():
            parts = []
            for e in range(expert):
                total = jnp.zeros((own, width), F32)
                for s in range(seq):
                    total += back_ref[s * expert + e].astype(F32)
                parts.append(total)
            table[...] = jnp.concatenate(parts, axis=0).astype(BF16)

        out_ref[...] = lax.dot_general(
            combine_ref[...],
            table[...],
            (((0,), (0,)), ((), ())),
            preferred_element_type=F32,
        )

    return pl.pallas_call(
        kernel,
        grid=(count // BLOCK,),
        out_shape=jax.ShapeDtypeStruct((count, width), F32),
        in_specs=[
            pl.BlockSpec((slots, BLOCK), lambda i: (0, i)),
            pl.BlockSpec(back.shape, lambda i: (0, 0, 0)),
        ],
        out_specs=pl.BlockSpec((BLOCK, width), lambda i: (i, 0)),
        scratch_shapes=[pltpu.VMEM((slots, width), BF16)],
        compiler_params=pltpu.CompilerParams(vmem_limit_bytes=16 * 2**20),
        cost_estimate=pl.CostEstimate(
            flops=2 * slots * count * width, bytes_accessed=4 * count * width, transcendentals=0
        ),
        name="mix",
    )(combine, back)


def local(tokens, slot_keys, w_in, w_out):
    seq = lax.axis_size("seq")
    expert = lax.axis_size("expert")
    group = ("seq", "expert")
    slots = slot_keys.shape[1]
    width = tokens.shape[1]
    own = slots // expert

    logits = full_logits(tokens, slot_keys)
    top = jnp.max(logits, axis=1)
    dispatch = jnp.exp(logits - top[:, None]).astype(BF16)
    combine = jax.nn.softmax(logits, axis=0).astype(BF16)
    totals = jnp.sum(dispatch.astype(F32), axis=1)
    weighted = jnp.dot(dispatch, tokens, preferred_element_type=F32)
    mean = (weighted / totals[:, None]).astype(BF16)
    weight = jnp.stack(spread(top + jnp.log(totals)), axis=1).astype(BF16)
    weight = jnp.pad(weight, ((0, 0), (0, LANES - weight.shape[1])))
    send = jnp.concatenate([mean, weight], axis=1).reshape(1, expert, own, width + LANES)
    send = jnp.broadcast_to(send, (seq, expert, own, width + LANES))
    got = lax.all_to_all(send.reshape(seq * expert, own, width + LANES), group, 0, 0)

    back = experts(got, w_in, w_out, seq, expert)
    back = lax.all_to_all(back, group, 0, 0)
    return mix(combine, back, seq, expert)


def solution(mesh):
    return jax.shard_map(
        local,
        mesh=mesh,
        in_specs=(
            P(("clip", "seq"), "expert"),
            P("expert", None),
            P("expert", None, "seq"),
            P("expert", "seq", None),
        ),
        out_specs=P(("clip", "seq"), "expert"),
        check_vma=False,
    )
```

```python
import jax
import jax.numpy as jnp
from jax import lax
from jax.experimental import pallas as pl
from jax.experimental.pallas import tpu as pltpu
from jax.sharding import PartitionSpec as P

BF16 = jnp.bfloat16
F32 = jnp.float32
LANES = 128
REACH = 125.0
BLOCK = 512


def swap(value, z_step, core_step):
    pairs = [
        (z * 2 + c, (z ^ z_step) * 2 + (c ^ core_step)) for z in range(2) for c in range(2)
    ]
    return lax.ppermute(value, "expert", pairs)


def spread(value):
    first = lax.reduce_precision(value, 8, 7)
    second = lax.reduce_precision(value - first, 8, 7)
    return [first, second, value - first - second]


def exchanged(scores, w_in, w_out):
    high = jnp.max(scores, axis=1)
    low = jnp.min(scores, axis=1)
    center = 0.5 * (high + low)
    span = jnp.maximum(high - low, 1e-30)
    code = jnp.exp2((scores - center[:, None]) * (2 * REACH / span)[:, None])
    side = jnp.stack(spread(center) + spread(span), axis=1)
    side = jnp.pad(side, ((0, 0), (0, LANES - side.shape[1])))
    sent = jnp.concatenate([code, side], axis=1).astype(BF16)
    sent, w_in, w_out = lax.optimization_barrier((sent, w_in, w_out))
    got = swap(sent, 1, 0)
    w_in, w_out = staged(w_in, w_out)
    got, w_in, w_out = lax.optimization_barrier((got, w_in, w_out))
    got = got.astype(F32)
    count = scores.shape[1]
    center = jnp.sum(got[:, count : count + 3], axis=1, keepdims=True)
    span = jnp.sum(got[:, count + 3 : count + 6], axis=1, keepdims=True)
    return jnp.log2(got[:, :count]) * (span / (2 * REACH)) + center, w_in, w_out


def scores(tokens, slot_keys):
    count, width = tokens.shape
    slots = slot_keys.shape[1]
    half = count // 2
    steps = half // BLOCK

    def kernel(keys_hbm, tokens_ref, theirs_ref, mine_ref, held_ref, keys_ref, sems):
        core = lax.axis_index("expert") % 2

        def rows(step):
            start = (1 - core) * half if step < steps else core * half
            return pl.ds(pl.multiple_of(start + (step % steps) * BLOCK, BLOCK), BLOCK)

        def copy(step):
            return pltpu.make_async_copy(
                tokens_ref.at[rows(step)], held_ref.at[rows(step)], sems.at[step]
            )

        keys = pltpu.make_async_copy(keys_hbm, keys_ref, sems.at[2 * steps])
        keys.start()
        for step in range(2 * steps):
            copy(step).start()
        keys.wait()
        for step in range(2 * steps):
            copy(step).wait()
            part = lax.dot_general(
                keys_ref[...],
                held_ref[rows(step)],
                (((1,), (1,)), ((), ())),
                preferred_element_type=F32,
            )
            target = theirs_ref if step < steps else mine_ref
            target[:, (step % steps) * BLOCK : (step % steps + 1) * BLOCK] = part

    whole = pl.BlockSpec(memory_space=pltpu.VMEM)
    return pl.pallas_call(
        kernel,
        out_shape=(
            jax.ShapeDtypeStruct((slots, half), F32),
            jax.ShapeDtypeStruct((slots, half), F32),
            pltpu.VMEM((count, width), BF16),
        ),
        in_specs=[pl.BlockSpec(memory_space=pltpu.HBM)] * 2,
        out_specs=(whole, whole, whole),
        scratch_shapes=[
            pltpu.VMEM((slots, width), BF16),
            pltpu.SemaphoreType.DMA((2 * steps + 1,)),
        ],
        compiler_params=pltpu.CompilerParams(vmem_limit_bytes=16 * 2**20),
        cost_estimate=pl.CostEstimate(
            flops=2 * slots * count * width, bytes_accessed=2 * count * width, transcendentals=0
        ),
        name="scores",
    )(
        pltpu.with_memory_space_constraint(slot_keys.T, pltpu.HBM),
        pltpu.with_memory_space_constraint(tokens, pltpu.HBM),
    )


def staged(first, second):
    pieces = first.shape[0]

    def kernel(first_ref, second_ref, first_out, second_out, sems):
        copies = []
        for i in range(pieces):
            copies.append(
                pltpu.make_async_copy(first_ref.at[i], first_out.at[i], sems.at[0, i])
            )
            copies.append(
                pltpu.make_async_copy(second_ref.at[i], second_out.at[i], sems.at[1, i])
            )
        for item in copies:
            item.start()
        for item in copies:
            item.wait()

    outside = pl.BlockSpec(memory_space=pltpu.HBM)
    whole = pl.BlockSpec(memory_space=pltpu.VMEM)
    return pl.pallas_call(
        kernel,
        out_shape=(pltpu.VMEM(first.shape, first.dtype), pltpu.VMEM(second.shape, second.dtype)),
        in_specs=[outside, outside],
        out_specs=(whole, whole),
        scratch_shapes=[pltpu.SemaphoreType.DMA((2, pieces))],
        compiler_params=pltpu.CompilerParams(vmem_limit_bytes=16 * 2**20),
        cost_estimate=pl.CostEstimate(
            flops=0, bytes_accessed=4 * (first.size + second.size), transcendentals=0
        ),
        name="staged",
    )(
        pltpu.with_memory_space_constraint(first, pltpu.HBM),
        pltpu.with_memory_space_constraint(second, pltpu.HBM),
    )


def full_logits(theirs, mine, w_in, w_out):
    core = lax.axis_index("expert") % 2
    mine = mine + swap(theirs, 0, 1)
    gained, w_in, w_out = exchanged(mine, w_in, w_out)
    mine = mine + gained
    other = swap(mine, 0, 1)
    logits = jnp.concatenate(
        [jnp.where(core == 0, mine, other), jnp.where(core == 0, other, mine)], axis=1
    )
    return logits, w_in, w_out


def experts(got, w_in, w_out, seq, expert):
    own, width = w_in.shape[0], w_in.shape[1] // expert
    hidden_width = w_in.shape[2]

    def kernel(got_ref, w_in_ref, w_out_ref, out_ref):
        weight = jnp.sum(got_ref[:, :, width:].astype(F32), axis=-1, keepdims=True)
        weight = weight.reshape(seq, expert, own, 1)
        scale = jnp.exp(weight - jnp.max(weight, axis=0, keepdims=True))
        scale = scale / jnp.sum(scale, axis=0, keepdims=True)
        pieces = []
        for e in range(expert):
            total = jnp.zeros((own, width), F32)
            for s in range(seq):
                total += got_ref[s * expert + e, :, :width].astype(F32) * scale[s, e]
            pieces.append(total.astype(BF16))
        rows = lax.broadcasted_iota(jnp.int32, (own, hidden_width), 0)
        inner = jnp.zeros((own, hidden_width), F32)
        for i in range(own):
            total = jnp.zeros((own, hidden_width), F32)
            for e in range(expert):
                total += jnp.dot(
                    pieces[e],
                    w_in_ref[i, e * width : (e + 1) * width, :],
                    preferred_element_type=F32,
                )
            inner = jnp.where(rows == i, total, inner)
        hidden = 0.5 * inner * (1.0 + lax.erf(inner * (0.5**0.5)))
        hidden = hidden.astype(BF16)
        for e in range(expert):
            rows = lax.broadcasted_iota(jnp.int32, (own, width), 0)
            result = jnp.zeros((own, width), F32)
            for i in range(own):
                part = jnp.dot(
                    hidden,
                    w_out_ref[i, :, e * width : (e + 1) * width],
                    preferred_element_type=F32,
                )
                result = jnp.where(rows == i, part, result)
            result = result.astype(BF16)
            for s in range(seq):
                out_ref[s * expert + e] = result

    whole = pl.BlockSpec(memory_space=pltpu.VMEM)
    return pl.pallas_call(
        kernel,
        out_shape=jax.ShapeDtypeStruct((seq * expert, own, width), BF16),
        in_specs=[whole, whole, whole],
        out_specs=whole,
        compiler_params=pltpu.CompilerParams(vmem_limit_bytes=24 * 2**20),
        cost_estimate=pl.CostEstimate(
            flops=4 * own * width * expert * hidden_width * own,
            bytes_accessed=2 * (w_in.size + w_out.size),
            transcendentals=own * hidden_width,
        ),
        name="experts",
    )(
        got,
        pltpu.with_memory_space_constraint(w_in, pltpu.VMEM),
        pltpu.with_memory_space_constraint(w_out, pltpu.VMEM),
    )


def local(tokens, slot_keys, w_in, w_out):
    seq = lax.axis_size("seq")
    expert = lax.axis_size("expert")
    group = ("seq", "expert")
    slots = slot_keys.shape[1]
    width = tokens.shape[1]
    own = slots // expert

    theirs, mine, tokens = scores(tokens, slot_keys)
    logits, w_in, w_out = full_logits(theirs, mine, w_in, w_out)
    top = jnp.max(logits, axis=1)
    dispatch = jnp.exp(logits - top[:, None]).astype(BF16)
    combine = jax.nn.softmax(logits, axis=0).astype(BF16)
    totals = jnp.sum(dispatch.astype(F32), axis=1)
    weighted = jnp.dot(dispatch, tokens, preferred_element_type=F32)
    mean = (weighted / totals[:, None]).astype(BF16)
    weight = jnp.stack(spread(top + jnp.log(totals)), axis=1).astype(BF16)
    weight = jnp.pad(weight, ((0, 0), (0, LANES - weight.shape[1])))
    send = jnp.concatenate([mean, weight], axis=1).reshape(1, expert, own, width + LANES)
    send = jnp.broadcast_to(send, (seq, expert, own, width + LANES))
    got = lax.all_to_all(send.reshape(seq * expert, own, width + LANES), group, 0, 0)

    back = experts(got, w_in, w_out, seq, expert)
    back = lax.all_to_all(back, group, 0, 0)
    returned = jnp.sum(back.reshape(seq, slots, width).astype(F32), axis=0).astype(BF16)
    return lax.dot_general(
        combine, returned, (((0,), (0,)), ((), ())), preferred_element_type=F32
    )


def solution(mesh):
    return jax.shard_map(
        local,
        mesh=mesh,
        in_specs=(
            P(("clip", "seq"), "expert"),
            P("expert", None),
            P("expert", None, "seq"),
            P("expert", "seq", None),
        ),
        out_specs=P(("clip", "seq"), "expert"),
        check_vma=False,
    )
```

```python
import jax
import jax.numpy as jnp
from jax import lax
from jax.experimental import pallas as pl
from jax.experimental.pallas import tpu as pltpu
from jax.sharding import PartitionSpec as P

BF16 = jnp.bfloat16
F32 = jnp.float32
LANES = 128
REACH = 125.0
BLOCK = 512
LIMIT = 16 * 2**20


def swap(value, z_step, core_step):
    pairs = [
        (z * 2 + c, (z ^ z_step) * 2 + (c ^ core_step)) for z in range(2) for c in range(2)
    ]
    return lax.ppermute(value, "expert", pairs)


def spread(value, lane, first):
    high = value.astype(BF16).astype(F32)
    middle = (value - high).astype(BF16).astype(F32)
    low = value - high - middle
    parts = jnp.where(lane == first, high, 0.0)
    parts = jnp.where(lane == first + 1, middle, parts)
    return jnp.where(lane == first + 2, low, parts)


def call(kernel, name, out_shape, inputs, flops=0, scratch=()):
    whole = pl.BlockSpec(memory_space=pltpu.VMEM)
    moved = sum(a.size * a.dtype.itemsize for a in inputs)
    return pl.pallas_call(
        kernel,
        out_shape=out_shape,
        in_specs=[whole] * len(inputs),
        out_specs=jax.tree.map(lambda _: whole, out_shape),
        scratch_shapes=scratch,
        compiler_params=pltpu.CompilerParams(vmem_limit_bytes=LIMIT),
        cost_estimate=pl.CostEstimate(flops=flops, bytes_accessed=moved, transcendentals=0),
        name=name,
    )(*inputs)


def encode(mine, gained):
    slots, count = mine.shape

    def kernel(mine_ref, gained_ref, total_ref, code_ref):
        total = mine_ref[...] + gained_ref[...]
        total_ref[...] = total
        high = jnp.max(total, axis=1, keepdims=True)
        low = jnp.min(total, axis=1, keepdims=True)
        center = 0.5 * (high + low)
        span = jnp.maximum(high - low, 1e-30)
        code = jnp.exp2((total - center) * (2 * REACH / span))
        code_ref[:, :count] = code.astype(BF16)
        lane = lax.broadcasted_iota(jnp.int32, (slots, LANES), 1)
        side = spread(center, lane, 0) + spread(span, lane, 3)
        code_ref[:, count:] = side.astype(BF16)

    return call(
        kernel,
        "encode",
        (
            jax.ShapeDtypeStruct((slots, count), F32),
            jax.ShapeDtypeStruct((slots, count + LANES), BF16),
        ),
        (mine, gained),
    )


def decode(total, code):
    slots, count = total.shape

    def kernel(total_ref, code_ref, out_ref):
        side = code_ref[:, count:].astype(F32)
        lane = lax.broadcasted_iota(jnp.int32, (slots, LANES), 1)
        center = jnp.sum(jnp.where(lane < 3, side, 0.0), axis=1, keepdims=True)
        span = jnp.sum(jnp.where(lane < 3, 0.0, side), axis=1, keepdims=True)
        power = jnp.log2(code_ref[:, :count].astype(F32))
        out_ref[...] = total_ref[...] + (power * (span / (2 * REACH)) + center)

    return call(
        kernel, "decode", jax.ShapeDtypeStruct((slots, count), F32), (total, code)
    )


def weigh(mine, other, tokens, seq, expert):
    slots, half = mine.shape
    width = tokens.shape[1]
    own = slots // expert

    def kernel(mine_ref, other_ref, tokens_ref, send_ref, combine_ref):
        core = lax.axis_index("expert") % 2
        places = [
            pl.ds(pl.multiple_of(start, half), half) for start in (core * half, (1 - core) * half)
        ]
        parts = [mine_ref[...], other_ref[...]]
        top = jnp.max(jnp.maximum(parts[0], parts[1]), axis=1, keepdims=True)
        totals = jnp.zeros((slots, 1), F32)
        weighted = jnp.zeros((slots, width), F32)
        for part, place in zip(parts, places):
            dispatch = jnp.exp(part - top).astype(BF16)
            totals += jnp.sum(dispatch.astype(F32), axis=1, keepdims=True)
            weighted += jnp.dot(dispatch, tokens_ref[place, :], preferred_element_type=F32)
            shifted = jnp.exp(part - jnp.max(part, axis=0, keepdims=True))
            share = shifted / jnp.sum(shifted, axis=0, keepdims=True)
            combine_ref[:, place] = share.astype(BF16)
        lane = lax.broadcasted_iota(jnp.int32, (slots, LANES), 1)
        weight = spread(top + jnp.log(totals), lane, 0)
        block = jnp.concatenate([weighted / totals, weight], axis=1)
        for e in range(expert):
            piece = block[e * own : (e + 1) * own].astype(BF16)
            for s in range(seq):
                send_ref[s * expert + e] = piece

    return call(
        kernel,
        "weigh",
        (
            jax.ShapeDtypeStruct((seq * expert, own, width + LANES), BF16),
            jax.ShapeDtypeStruct((slots, 2 * half), BF16),
        ),
        (mine, other, tokens),
        flops=4 * slots * half * width,
    )


def scores(tokens, slot_keys):
    count, width = tokens.shape
    slots = slot_keys.shape[1]
    half = count // 2
    steps = half // BLOCK

    def kernel(keys_hbm, tokens_ref, theirs_ref, mine_ref, held_ref, keys_ref, sems):
        core = lax.axis_index("expert") % 2

        def rows(step):
            start = (1 - core) * half if step < steps else core * half
            return pl.ds(pl.multiple_of(start + (step % steps) * BLOCK, BLOCK), BLOCK)

        def copy(step):
            return pltpu.make_async_copy(
                tokens_ref.at[rows(step)], held_ref.at[rows(step)], sems.at[step]
            )

        keys = pltpu.make_async_copy(keys_hbm, keys_ref, sems.at[2 * steps])
        keys.start()
        for step in range(2 * steps):
            copy(step).start()
        keys.wait()
        for step in range(2 * steps):
            copy(step).wait()
            part = lax.dot_general(
                keys_ref[...],
                held_ref[rows(step)],
                (((1,), (1,)), ((), ())),
                preferred_element_type=F32,
            )
            target = theirs_ref if step < steps else mine_ref
            target[:, (step % steps) * BLOCK : (step % steps + 1) * BLOCK] = part

    whole = pl.BlockSpec(memory_space=pltpu.VMEM)
    return pl.pallas_call(
        kernel,
        out_shape=(
            jax.ShapeDtypeStruct((slots, half), F32),
            jax.ShapeDtypeStruct((slots, half), F32),
            pltpu.VMEM((count, width), BF16),
        ),
        in_specs=[pl.BlockSpec(memory_space=pltpu.HBM)] * 2,
        out_specs=(whole, whole, whole),
        scratch_shapes=[
            pltpu.VMEM((slots, width), BF16),
            pltpu.SemaphoreType.DMA((2 * steps + 1,)),
        ],
        compiler_params=pltpu.CompilerParams(vmem_limit_bytes=LIMIT),
        cost_estimate=pl.CostEstimate(
            flops=2 * slots * count * width, bytes_accessed=2 * count * width, transcendentals=0
        ),
        name="scores",
    )(
        pltpu.with_memory_space_constraint(slot_keys.T, pltpu.HBM),
        pltpu.with_memory_space_constraint(tokens, pltpu.HBM),
    )


def staged(first, second):
    pieces = first.shape[0]

    def kernel(first_ref, second_ref, first_out, second_out, sems):
        copies = []
        for i in range(pieces):
            copies.append(
                pltpu.make_async_copy(first_ref.at[i], first_out.at[i], sems.at[0, i])
            )
            copies.append(
                pltpu.make_async_copy(second_ref.at[i], second_out.at[i], sems.at[1, i])
            )
        for item in copies:
            item.start()
        for item in copies:
            item.wait()

    outside = pl.BlockSpec(memory_space=pltpu.HBM)
    whole = pl.BlockSpec(memory_space=pltpu.VMEM)
    return pl.pallas_call(
        kernel,
        out_shape=(pltpu.VMEM(first.shape, first.dtype), pltpu.VMEM(second.shape, second.dtype)),
        in_specs=[outside, outside],
        out_specs=(whole, whole),
        scratch_shapes=[pltpu.SemaphoreType.DMA((2, pieces))],
        compiler_params=pltpu.CompilerParams(vmem_limit_bytes=LIMIT),
        cost_estimate=pl.CostEstimate(
            flops=0, bytes_accessed=4 * (first.size + second.size), transcendentals=0
        ),
        name="staged",
    )(
        pltpu.with_memory_space_constraint(first, pltpu.HBM),
        pltpu.with_memory_space_constraint(second, pltpu.HBM),
    )


def experts(got, w_in, w_out, seq, expert):
    own, width = w_in.shape[0], w_in.shape[1] // expert
    hidden_width = w_in.shape[2]

    def kernel(got_ref, w_in_ref, w_out_ref, out_ref):
        weight = jnp.sum(got_ref[:, :, width:].astype(F32), axis=-1, keepdims=True)
        weight = weight.reshape(seq, expert, own, 1)
        scale = jnp.exp(weight - jnp.max(weight, axis=0, keepdims=True))
        scale = scale / jnp.sum(scale, axis=0, keepdims=True)
        pieces = []
        for e in range(expert):
            total = jnp.zeros((own, width), F32)
            for s in range(seq):
                total += got_ref[s * expert + e, :, :width].astype(F32) * scale[s, e]
            pieces.append(total.astype(BF16))
        rows = lax.broadcasted_iota(jnp.int32, (own, hidden_width), 0)
        inner = jnp.zeros((own, hidden_width), F32)
        for i in range(own):
            total = jnp.zeros((own, hidden_width), F32)
            for e in range(expert):
                total += jnp.dot(
                    pieces[e],
                    w_in_ref[i, e * width : (e + 1) * width, :],
                    preferred_element_type=F32,
                )
            inner = jnp.where(rows == i, total, inner)
        hidden = 0.5 * inner * (1.0 + lax.erf(inner * (0.5**0.5)))
        hidden = hidden.astype(BF16)
        for e in range(expert):
            rows = lax.broadcasted_iota(jnp.int32, (own, width), 0)
            result = jnp.zeros((own, width), F32)
            for i in range(own):
                part = jnp.dot(
                    hidden,
                    w_out_ref[i, :, e * width : (e + 1) * width],
                    preferred_element_type=F32,
                )
                result = jnp.where(rows == i, part, result)
            result = result.astype(BF16)
            for s in range(seq):
                out_ref[s * expert + e] = result

    whole = pl.BlockSpec(memory_space=pltpu.VMEM)
    return pl.pallas_call(
        kernel,
        out_shape=jax.ShapeDtypeStruct((seq * expert, own, width), BF16),
        in_specs=[whole, whole, whole],
        out_specs=whole,
        compiler_params=pltpu.CompilerParams(vmem_limit_bytes=LIMIT),
        cost_estimate=pl.CostEstimate(
            flops=4 * own * width * expert * hidden_width * own,
            bytes_accessed=2 * (w_in.size + w_out.size),
            transcendentals=own * hidden_width,
        ),
        name="experts",
    )(
        got,
        pltpu.with_memory_space_constraint(w_in, pltpu.VMEM),
        pltpu.with_memory_space_constraint(w_out, pltpu.VMEM),
    )


def local(tokens, slot_keys, w_in, w_out):
    seq = lax.axis_size("seq")
    expert = lax.axis_size("expert")
    group = ("seq", "expert")
    slots = slot_keys.shape[1]
    width = tokens.shape[1]

    theirs, mine, tokens = scores(tokens, slot_keys)
    mine, sent = encode(mine, swap(theirs, 0, 1))
    sent, w_in, w_out = lax.optimization_barrier((sent, w_in, w_out))
    got = swap(sent, 1, 0)
    w_in, w_out = staged(w_in, w_out)
    got, w_in, w_out = lax.optimization_barrier((got, w_in, w_out))
    mine = decode(mine, got)
    send, combine = weigh(mine, swap(mine, 0, 1), tokens, seq, expert)
    got = lax.all_to_all(send, group, 0, 0)
    back = experts(got, w_in, w_out, seq, expert)
    back = lax.all_to_all(back, group, 0, 0)
    returned = jnp.sum(back.reshape(seq, slots, width).astype(F32), axis=0).astype(BF16)
    return lax.dot_general(
        combine, returned, (((0,), (0,)), ((), ())), preferred_element_type=F32
    )


def solution(mesh):
    return jax.shard_map(
        local,
        mesh=mesh,
        in_specs=(
            P(("clip", "seq"), "expert"),
            P("expert", None),
            P("expert", None, "seq"),
            P("expert", "seq", None),
        ),
        out_specs=P(("clip", "seq"), "expert"),
        check_vma=False,
    )
```

```python
import jax
import jax.numpy as jnp
from jax import lax
from jax.experimental import pallas as pl
from jax.experimental.pallas import tpu as pltpu
from jax.sharding import PartitionSpec as P

BF16 = jnp.bfloat16
F32 = jnp.float32
LANES = 128
REACH = 125.0
BLOCK = 512
MIX = 512
LIMIT = 16 * 2**20


def swap(value, z_step, core_step):
    pairs = [
        (z * 2 + c, (z ^ z_step) * 2 + (c ^ core_step)) for z in range(2) for c in range(2)
    ]
    return lax.ppermute(value, "expert", pairs)


def spread(value, lane, first):
    high = value.astype(BF16).astype(F32)
    middle = (value - high).astype(BF16).astype(F32)
    low = value - high - middle
    parts = jnp.where(lane == first, high, 0.0)
    parts = jnp.where(lane == first + 1, middle, parts)
    return jnp.where(lane == first + 2, low, parts)


def call(kernel, name, out_shape, inputs, flops=0, scratch=()):
    whole = pl.BlockSpec(memory_space=pltpu.VMEM)
    moved = sum(a.size * a.dtype.itemsize for a in inputs)
    return pl.pallas_call(
        kernel,
        out_shape=out_shape,
        in_specs=[whole] * len(inputs),
        out_specs=jax.tree.map(lambda _: whole, out_shape),
        scratch_shapes=scratch,
        compiler_params=pltpu.CompilerParams(vmem_limit_bytes=LIMIT),
        cost_estimate=pl.CostEstimate(flops=flops, bytes_accessed=moved, transcendentals=0),
        name=name,
    )(*inputs)


def encode(mine, gained):
    slots, count = mine.shape

    def kernel(mine_ref, gained_ref, total_ref, code_ref):
        total = mine_ref[...] + gained_ref[...]
        total_ref[...] = total
        high = jnp.max(total, axis=1, keepdims=True)
        low = jnp.min(total, axis=1, keepdims=True)
        center = 0.5 * (high + low)
        span = jnp.maximum(high - low, 1e-30)
        code = jnp.exp2((total - center) * (2 * REACH / span))
        code_ref[:, :count] = code.astype(BF16)
        lane = lax.broadcasted_iota(jnp.int32, (slots, LANES), 1)
        side = spread(center, lane, 0) + spread(span, lane, 3)
        code_ref[:, count:] = side.astype(BF16)

    return call(
        kernel,
        "encode",
        (
            jax.ShapeDtypeStruct((slots, count), F32),
            jax.ShapeDtypeStruct((slots, count + LANES), BF16),
        ),
        (mine, gained),
    )


def decoded(total, code):
    count = total.shape[1]
    side = code[:, count:].astype(F32)
    lane = lax.broadcasted_iota(jnp.int32, side.shape, 1)
    center = jnp.sum(jnp.where(lane < 3, side, 0.0), axis=1, keepdims=True)
    span = jnp.sum(jnp.where(lane < 3, 0.0, side), axis=1, keepdims=True)
    power = jnp.log2(code[:, :count].astype(F32))
    return total + (power * (span / (2 * REACH)) + center)


def weigh(totals_of, codes, held, seq, expert):
    slots, half = totals_of[0].shape
    width = held[0].shape[1]
    own = slots // expert

    def kernel(mine_ref, other_ref, code_ref, sent_ref, near_ref, far_ref, send_ref, combine_ref):
        core = lax.axis_index("expert") % 2
        places = [
            pl.ds(pl.multiple_of(start, half), half) for start in (core * half, (1 - core) * half)
        ]
        parts = [decoded(mine_ref[...], code_ref[...]), decoded(other_ref[...], sent_ref[...])]
        top = jnp.max(jnp.maximum(parts[0], parts[1]), axis=1, keepdims=True)
        totals = jnp.zeros((slots, 1), F32)
        weighted = jnp.zeros((slots, width), F32)
        for part, place, held_ref in zip(parts, places, (near_ref, far_ref)):
            dispatch = jnp.exp(part - top).astype(BF16)
            totals += jnp.sum(dispatch.astype(F32), axis=1, keepdims=True)
            weighted += jnp.dot(dispatch, held_ref[...], preferred_element_type=F32)
            shifted = jnp.exp(part - jnp.max(part, axis=0, keepdims=True))
            share = shifted / jnp.sum(shifted, axis=0, keepdims=True)
            combine_ref[:, place] = share.astype(BF16)
        lane = lax.broadcasted_iota(jnp.int32, (slots, LANES), 1)
        weight = top + jnp.log(totals)
        first, second = spread(weight, lane, 0), spread(weight, lane, 3)
        mean = weighted / totals
        for e in range(expert):
            near = slice(e * own, e * own + own // 2)
            far = slice(e * own + own // 2, (e + 1) * own)
            piece = [mean[near], mean[far], first[near] + second[far]]
            piece = jnp.concatenate(piece, axis=1).astype(BF16)
            for s in range(seq):
                send_ref[s * expert + e] = piece

    return call(
        kernel,
        "weigh",
        (
            jax.ShapeDtypeStruct((seq * expert, own // 2, 2 * width + LANES), BF16),
            jax.ShapeDtypeStruct((slots, 2 * half), BF16),
        ),
        (*totals_of, *codes, *held),
        flops=4 * slots * half * width,
    )


def scores(tokens, slot_keys, mine):
    count, width = tokens.shape
    slots = slot_keys.shape[1]
    half = count // 2
    steps = half // BLOCK

    def kernel(keys_hbm, tokens_ref, part_ref, held_ref, keys_ref, sems):
        core = lax.axis_index("expert") % 2
        start = (core if mine else 1 - core) * half
        copies = []
        for step in range(steps):
            source = pl.ds(pl.multiple_of(start + step * BLOCK, BLOCK), BLOCK)
            target = pl.ds(step * BLOCK, BLOCK)
            copies.append(
                pltpu.make_async_copy(
                    tokens_ref.at[source], held_ref.at[target], sems.at[step]
                )
            )
        keys = pltpu.make_async_copy(keys_hbm, keys_ref, sems.at[steps])
        keys.start()
        for copy in copies:
            copy.start()
        keys.wait()
        for step in range(steps):
            copies[step].wait()
            target = pl.ds(step * BLOCK, BLOCK)
            part_ref[:, target] = lax.dot_general(
                keys_ref[...],
                held_ref[target],
                (((1,), (1,)), ((), ())),
                preferred_element_type=F32,
            )

    whole = pl.BlockSpec(memory_space=pltpu.VMEM)
    return pl.pallas_call(
        kernel,
        out_shape=(
            jax.ShapeDtypeStruct((slots, half), F32),
            pltpu.VMEM((half, width), BF16),
        ),
        in_specs=[pl.BlockSpec(memory_space=pltpu.HBM)] * 2,
        out_specs=(whole, whole),
        scratch_shapes=[
            pltpu.VMEM((slots, width), BF16),
            pltpu.SemaphoreType.DMA((steps + 1,)),
        ],
        compiler_params=pltpu.CompilerParams(vmem_limit_bytes=LIMIT),
        cost_estimate=pl.CostEstimate(
            flops=2 * slots * half * width, bytes_accessed=4 * half * width, transcendentals=0
        ),
        name="scores_mine" if mine else "scores_theirs",
    )(
        pltpu.with_memory_space_constraint(slot_keys.T, pltpu.HBM),
        pltpu.with_memory_space_constraint(tokens, pltpu.HBM),
    )


def staged(first, second):
    pieces = first.shape[0]

    def kernel(first_ref, second_ref, first_out, second_out, sems):
        copies = []
        for i in range(pieces):
            copies.append(
                pltpu.make_async_copy(first_ref.at[i], first_out.at[i], sems.at[0, i])
            )
            copies.append(
                pltpu.make_async_copy(second_ref.at[i], second_out.at[i], sems.at[1, i])
            )
        for item in copies:
            item.start()
        for item in copies:
            item.wait()

    outside = pl.BlockSpec(memory_space=pltpu.HBM)
    whole = pl.BlockSpec(memory_space=pltpu.VMEM)
    return pl.pallas_call(
        kernel,
        out_shape=(pltpu.VMEM(first.shape, first.dtype), pltpu.VMEM(second.shape, second.dtype)),
        in_specs=[outside, outside],
        out_specs=(whole, whole),
        scratch_shapes=[pltpu.SemaphoreType.DMA((2, pieces))],
        compiler_params=pltpu.CompilerParams(vmem_limit_bytes=LIMIT),
        cost_estimate=pl.CostEstimate(
            flops=0, bytes_accessed=4 * (first.size + second.size), transcendentals=0
        ),
        name="staged",
    )(
        pltpu.with_memory_space_constraint(first, pltpu.HBM),
        pltpu.with_memory_space_constraint(second, pltpu.HBM),
    )


def experts(got, w_in, w_out, seq, expert):
    own, width = w_in.shape[0], w_in.shape[1] // expert
    hidden_width = w_in.shape[2]

    def kernel(got_ref, w_in_ref, w_out_ref, out_ref):
        side = got_ref[:, :, 2 * width :].astype(F32)
        lane = lax.broadcasted_iota(jnp.int32, side.shape, 2)
        scales = []
        for wanted in (lane < 3, lane >= 3):
            weight = jnp.sum(jnp.where(wanted, side, 0.0), axis=-1, keepdims=True)
            weight = weight.reshape(seq, expert, own // 2, 1)
            scale = jnp.exp(weight - jnp.max(weight, axis=0, keepdims=True))
            scales.append(scale / jnp.sum(scale, axis=0, keepdims=True))
        pieces = []
        for e in range(expert):
            halves = []
            for k in range(2):
                total = jnp.zeros((own // 2, width), F32)
                for s in range(seq):
                    part = got_ref[s * expert + e, :, k * width : (k + 1) * width]
                    total += part.astype(F32) * scales[k][s, e]
                halves.append(total)
            pieces.append(jnp.concatenate(halves, axis=0).astype(BF16))
        rows = lax.broadcasted_iota(jnp.int32, (own, hidden_width), 0)
        inner = jnp.zeros((own, hidden_width), F32)
        for i in range(own):
            total = jnp.zeros((own, hidden_width), F32)
            for e in range(expert):
                total += jnp.dot(
                    pieces[e],
                    w_in_ref[i, e * width : (e + 1) * width, :],
                    preferred_element_type=F32,
                )
            inner = jnp.where(rows == i, total, inner)
        hidden = 0.5 * inner * (1.0 + lax.erf(inner * (0.5**0.5)))
        hidden = hidden.astype(BF16)
        for e in range(expert):
            rows = lax.broadcasted_iota(jnp.int32, (own, width), 0)
            result = jnp.zeros((own, width), F32)
            for i in range(own):
                part = jnp.dot(
                    hidden,
                    w_out_ref[i, :, e * width : (e + 1) * width],
                    preferred_element_type=F32,
                )
                result = jnp.where(rows == i, part, result)
            result = result.astype(BF16)
            for s in range(seq):
                out_ref[s * expert + e] = result

    whole = pl.BlockSpec(memory_space=pltpu.VMEM)
    return pl.pallas_call(
        kernel,
        out_shape=jax.ShapeDtypeStruct((seq * expert, own, width), BF16),
        in_specs=[whole, whole, whole],
        out_specs=whole,
        compiler_params=pltpu.CompilerParams(vmem_limit_bytes=LIMIT),
        cost_estimate=pl.CostEstimate(
            flops=4 * own * width * expert * hidden_width * own,
            bytes_accessed=2 * (w_in.size + w_out.size),
            transcendentals=own * hidden_width,
        ),
        name="experts",
    )(
        got,
        pltpu.with_memory_space_constraint(w_in, pltpu.VMEM),
        pltpu.with_memory_space_constraint(w_out, pltpu.VMEM),
    )


def mix(combine, back, seq, expert):
    slots, count = combine.shape
    own, width = back.shape[1:]
    steps = count // MIX

    def kernel(combine_ref, back_ref, out_ref, held_ref, sems):
        parts = []
        for e in range(expert):
            total = jnp.zeros((own, width), F32)
            for s in range(seq):
                total += back_ref[s * expert + e].astype(F32)
            parts.append(total)
        table = jnp.concatenate(parts, axis=0).astype(BF16)
        copies = []
        for step in range(steps):
            rows = pl.ds(step * MIX, MIX)
            held_ref[rows, :] = lax.dot_general(
                combine_ref[:, rows], table, (((0,), (0,)), ((), ())), preferred_element_type=F32
            )
            copy = pltpu.make_async_copy(held_ref.at[rows], out_ref.at[rows], sems.at[step])
            copy.start()
            copies.append(copy)
        for copy in copies:
            copy.wait()

    whole = pl.BlockSpec(memory_space=pltpu.VMEM)
    return pl.pallas_call(
        kernel,
        out_shape=jax.ShapeDtypeStruct((count, width), F32),
        in_specs=[whole, whole],
        out_specs=pl.BlockSpec(memory_space=pltpu.HBM),
        scratch_shapes=[
            pltpu.VMEM((count, width), F32),
            pltpu.SemaphoreType.DMA((steps,)),
        ],
        compiler_params=pltpu.CompilerParams(vmem_limit_bytes=LIMIT),
        cost_estimate=pl.CostEstimate(
            flops=2 * slots * count * width, bytes_accessed=4 * count * width, transcendentals=0
        ),
        name="mix",
    )(combine, back)


def local(tokens, slot_keys, w_in, w_out):
    seq = lax.axis_size("seq")
    expert = lax.axis_size("expert")
    group = ("seq", "expert")
    slots = slot_keys.shape[1]
    width = tokens.shape[1]

    theirs, tokens_other = scores(tokens, slot_keys, False)
    theirs, tokens = lax.optimization_barrier((theirs, tokens))
    gained = swap(theirs, 0, 1)
    mine, tokens_mine = scores(tokens, slot_keys, True)
    gained, mine = lax.optimization_barrier((gained, mine))
    mine, sent = encode(mine, gained)
    sent, mine, w_in, w_out = lax.optimization_barrier((sent, mine, w_in, w_out))
    code = swap(sent, 1, 0)
    other = swap(mine, 0, 1)
    w_in, w_out = staged(w_in, w_out)
    code, other, w_in, w_out = lax.optimization_barrier((code, other, w_in, w_out))
    codes = (code, swap(code, 0, 1))
    held = (tokens_mine, tokens_other)
    send, combine = weigh((mine, other), codes, held, seq, expert)
    got = lax.all_to_all(send, group, 0, 0)
    back = experts(got, w_in, w_out, seq, expert)
    back = lax.all_to_all(back, group, 0, 0)
    return mix(combine, back, seq, expert)


def solution(mesh):
    return jax.shard_map(
        local,
        mesh=mesh,
        in_specs=(
            P(("clip", "seq"), "expert"),
            P("expert", None),
            P("expert", None, "seq"),
            P("expert", "seq", None),
        ),
        out_specs=P(("clip", "seq"), "expert"),
        check_vma=False,
    )
```

```python
import jax
import jax.numpy as jnp
from jax import lax
from jax.experimental import pallas as pl
from jax.experimental.pallas import tpu as pltpu
from jax.sharding import PartitionSpec as P

BF16 = jnp.bfloat16
F32 = jnp.float32
LANES = 128
REACH = 125.0
BLOCK = 1024
MIX = 512
LIMIT = 16 * 2**20


def swap(value, axis):
    return lax.ppermute(value, axis, [(0, 1), (1, 0)])


def spread(value, lane, first):
    high = value.astype(BF16).astype(F32)
    middle = (value - high).astype(BF16).astype(F32)
    low = value - high - middle
    parts = jnp.where(lane == first, high, 0.0)
    parts = jnp.where(lane == first + 1, middle, parts)
    return jnp.where(lane == first + 2, low, parts)


def call(kernel, name, out_shape, inputs, flops=0, scratch=()):
    whole = pl.BlockSpec(memory_space=pltpu.VMEM)
    moved = sum(a.size * a.dtype.itemsize for a in inputs)
    return pl.pallas_call(
        kernel,
        out_shape=out_shape,
        in_specs=[whole] * len(inputs),
        out_specs=jax.tree.map(lambda _: whole, out_shape),
        scratch_shapes=scratch,
        compiler_params=pltpu.CompilerParams(vmem_limit_bytes=LIMIT),
        cost_estimate=pl.CostEstimate(flops=flops, bytes_accessed=moved, transcendentals=0),
        name=name,
    )(*inputs)


def encode(mine, gained):
    slots, count = mine.shape

    def kernel(mine_ref, gained_ref, total_ref, code_ref):
        total = mine_ref[...] + gained_ref[...]
        total_ref[...] = total
        high = jnp.max(total, axis=1, keepdims=True)
        low = jnp.min(total, axis=1, keepdims=True)
        center = 0.5 * (high + low)
        span = jnp.maximum(high - low, 1e-30)
        code = jnp.exp2((total - center) * (2 * REACH / span))
        code_ref[:, :count] = code.astype(BF16)
        lane = lax.broadcasted_iota(jnp.int32, (slots, LANES), 1)
        side = spread(center, lane, 0) + spread(span, lane, 3)
        code_ref[:, count:] = side.astype(BF16)

    return call(
        kernel,
        "encode",
        (
            jax.ShapeDtypeStruct((slots, count), F32),
            jax.ShapeDtypeStruct((slots, count + LANES), BF16),
        ),
        (mine, gained),
    )


def decoded(total, code):
    count = total.shape[1]
    side = code[:, count:].astype(F32)
    lane = lax.broadcasted_iota(jnp.int32, side.shape, 1)
    center = jnp.sum(jnp.where(lane < 3, side, 0.0), axis=1, keepdims=True)
    span = jnp.sum(jnp.where(lane < 3, 0.0, side), axis=1, keepdims=True)
    power = jnp.log2(code[:, :count].astype(F32))
    return total + (power * (span / (2 * REACH)) + center)


def weigh(totals_of, codes, held, seq, planes):
    slots, half = totals_of[0].shape
    width = held[0].shape[1]
    own = slots // planes // 2

    def kernel(mine_ref, other_ref, code_ref, sent_ref, *refs):
        near, far, near_next, far_next, send_ref, combine_ref = refs
        core = lax.axis_index("core")
        places = [
            pl.ds(pl.multiple_of(start, half), half) for start in (core * half, (1 - core) * half)
        ]
        parts = [decoded(mine_ref[...], code_ref[...]), decoded(other_ref[...], sent_ref[...])]
        first, second = [], []
        for part, place in zip(parts, places):
            shifted = jnp.exp(part - jnp.max(part, axis=0, keepdims=True))
            share = shifted / jnp.sum(shifted, axis=0, keepdims=True)
            combine_ref[:, place] = share.astype(BF16)
            rows = [part[k * own : (k + 1) * own] for k in range(2 * planes)]
            first += [jnp.where(core == 0, rows[2 * z], rows[2 * z + 1]) for z in range(planes)]
        parts = [jnp.concatenate(first[k * planes : (k + 1) * planes], axis=0) for k in range(2)]
        top = jnp.max(jnp.maximum(parts[0], parts[1]), axis=1, keepdims=True)
        dispatch = [jnp.exp(part - top).astype(BF16) for part in parts]
        totals = sum(jnp.sum(d.astype(F32), axis=1, keepdims=True) for d in dispatch)

        def gathered(a, b):
            return (
                jnp.dot(dispatch[0], a[...], preferred_element_type=F32)
                + jnp.dot(dispatch[1], b[...], preferred_element_type=F32)
            ) / totals

        ours, next_ours = gathered(near, far), gathered(near_next, far_next)
        mean = jnp.concatenate(
            [jnp.where(core == 0, ours, next_ours), jnp.where(core == 0, next_ours, ours)], axis=1
        )
        lane = lax.broadcasted_iota(jnp.int32, (planes * own, LANES), 1)
        weight = top + jnp.log(totals)
        first, second = spread(weight, lane, 0), spread(weight, lane, 3)
        for z in range(planes):
            near_rows = slice(z * own, z * own + own // 2)
            far_rows = slice(z * own + own // 2, (z + 1) * own)
            piece = [mean[near_rows], mean[far_rows], first[near_rows] + second[far_rows]]
            piece = jnp.concatenate(piece, axis=1).astype(BF16)
            for s in range(seq):
                send_ref[s * planes + z] = piece

    return call(
        kernel,
        "weigh",
        (
            jax.ShapeDtypeStruct((seq * planes, own // 2, 4 * width + LANES), BF16),
            jax.ShapeDtypeStruct((slots, 2 * half), BF16),
        ),
        (*totals_of, *codes, *held),
        flops=8 * planes * own * half * width,
    )


def scores(tokens, slot_keys, mine):
    count, width = tokens.shape
    slots = slot_keys.shape[1]
    half = count // 2
    steps = half // BLOCK

    def kernel(keys_hbm, tokens_ref, part_ref, held_ref, keys_ref, sems):
        core = lax.axis_index("core")
        start = (core if mine else 1 - core) * half
        copies = []
        for step in range(steps):
            source = pl.ds(pl.multiple_of(start + step * BLOCK, BLOCK), BLOCK)
            target = pl.ds(step * BLOCK, BLOCK)
            copies.append(
                pltpu.make_async_copy(
                    tokens_ref.at[source], held_ref.at[target], sems.at[step]
                )
            )
        keys = pltpu.make_async_copy(keys_hbm, keys_ref, sems.at[steps])
        keys.start()
        for copy in copies:
            copy.start()
        keys.wait()
        for step in range(steps):
            copies[step].wait()
            target = pl.ds(step * BLOCK, BLOCK)
            part_ref[:, target] = lax.dot_general(
                keys_ref[...],
                held_ref[target],
                (((1,), (1,)), ((), ())),
                preferred_element_type=F32,
            )

    whole = pl.BlockSpec(memory_space=pltpu.VMEM)
    return pl.pallas_call(
        kernel,
        out_shape=(
            jax.ShapeDtypeStruct((slots, half), F32),
            pltpu.VMEM((half, width), BF16),
        ),
        in_specs=[pl.BlockSpec(memory_space=pltpu.HBM)] * 2,
        out_specs=(whole, whole),
        scratch_shapes=[
            pltpu.VMEM((slots, width), BF16),
            pltpu.SemaphoreType.DMA((steps + 1,)),
        ],
        compiler_params=pltpu.CompilerParams(vmem_limit_bytes=LIMIT),
        cost_estimate=pl.CostEstimate(
            flops=2 * slots * half * width, bytes_accessed=4 * half * width, transcendentals=0
        ),
        name="scores_mine" if mine else "scores_theirs",
    )(
        pltpu.with_memory_space_constraint(slot_keys.T, pltpu.HBM),
        pltpu.with_memory_space_constraint(tokens, pltpu.HBM),
    )


def staged(first, second):
    pieces = first.shape[0]

    def kernel(first_ref, second_ref, first_out, second_out, sems):
        copies = []
        for i in range(pieces):
            copies.append(
                pltpu.make_async_copy(first_ref.at[i], first_out.at[i], sems.at[0, i])
            )
            copies.append(
                pltpu.make_async_copy(second_ref.at[i], second_out.at[i], sems.at[1, i])
            )
        for item in copies:
            item.start()
        for item in copies:
            item.wait()

    outside = pl.BlockSpec(memory_space=pltpu.HBM)
    whole = pl.BlockSpec(memory_space=pltpu.VMEM)
    return pl.pallas_call(
        kernel,
        out_shape=(pltpu.VMEM(first.shape, first.dtype), pltpu.VMEM(second.shape, second.dtype)),
        in_specs=[outside, outside],
        out_specs=(whole, whole),
        scratch_shapes=[pltpu.SemaphoreType.DMA((2, pieces))],
        compiler_params=pltpu.CompilerParams(vmem_limit_bytes=LIMIT),
        cost_estimate=pl.CostEstimate(
            flops=0, bytes_accessed=4 * (first.size + second.size), transcendentals=0
        ),
        name="staged",
    )(
        pltpu.with_memory_space_constraint(first, pltpu.HBM),
        pltpu.with_memory_space_constraint(second, pltpu.HBM),
    )


def projected(hidden, w_out_ref, core, planes, width):
    own = hidden.shape[0]
    rows = lax.broadcasted_iota(jnp.int32, (own, width), 0)
    results = []
    for z in range(planes):
        start = pl.multiple_of((2 * z + core) * width, width)
        result = jnp.zeros((own, width), F32)
        for i in range(own):
            part = jnp.dot(
                hidden, w_out_ref[i, :, pl.ds(start, width)], preferred_element_type=F32
            )
            result = jnp.where(rows == i, part, result)
        results.append(result.astype(BF16))
    return jnp.stack(results)


def kept(hidden, w_out, planes):
    own, width = w_out.shape[0], w_out.shape[2] // planes // 2

    def kernel(hidden_ref, w_out_ref, out_ref):
        core = lax.axis_index("core")
        out_ref[...] = projected(hidden_ref[...], w_out_ref, core, planes, width)

    return call(
        kernel,
        "kept",
        jax.ShapeDtypeStruct((planes, own, width), BF16),
        (hidden, pltpu.with_memory_space_constraint(w_out, pltpu.VMEM)),
        flops=16 * w_out.size,
    )


def packed(keep, taken, seq):
    planes, own, width = keep.shape

    def kernel(keep_ref, taken_ref, out_ref):
        for z in range(planes):
            pair = jnp.concatenate([keep_ref[z], taken_ref[z]], axis=0)
            for s in range(seq):
                out_ref[s * planes + z] = pair

    return call(
        kernel,
        "packed",
        jax.ShapeDtypeStruct((seq * planes, 2 * own, width), BF16),
        (keep, taken),
    )


def experts(got, w_in, w_out, seq, expert):
    own, width = w_in.shape[0], w_in.shape[1] // expert
    planes = expert // 2
    hidden_width = w_in.shape[2]

    def kernel(got_ref, w_in_ref, w_out_ref, hidden_ref, give_ref):
        side = got_ref[:, :, 4 * width :].astype(F32)
        lane = lax.broadcasted_iota(jnp.int32, side.shape, 2)
        scales = []
        for wanted in (lane < 3, lane >= 3):
            weight = jnp.sum(jnp.where(wanted, side, 0.0), axis=-1, keepdims=True)
            weight = weight.reshape(seq, planes, own // 2, 1)
            scale = jnp.exp(weight - jnp.max(weight, axis=0, keepdims=True))
            scales.append(scale / jnp.sum(scale, axis=0, keepdims=True))
        pieces = []
        for z in range(planes):
            halves = []
            for k in range(2):
                total = jnp.zeros((own // 2, 2 * width), F32)
                for s in range(seq):
                    part = got_ref[s * planes + z, :, 2 * k * width : 2 * (k + 1) * width]
                    total += part.astype(F32) * scales[k][s, z]
                halves.append(total)
            both = jnp.concatenate(halves, axis=0).astype(BF16)
            pieces += [both[:, :width], both[:, width:]]
        rows = lax.broadcasted_iota(jnp.int32, (own, hidden_width), 0)
        inner = jnp.zeros((own, hidden_width), F32)
        for i in range(own):
            total = jnp.zeros((own, hidden_width), F32)
            for e in range(expert):
                total += jnp.dot(
                    pieces[e],
                    w_in_ref[i, e * width : (e + 1) * width, :],
                    preferred_element_type=F32,
                )
            inner = jnp.where(rows == i, total, inner)
        hidden = 0.5 * inner * (1.0 + lax.erf(inner * (0.5**0.5)))
        hidden = hidden.astype(BF16)
        hidden_ref[...] = hidden
        core = lax.axis_index("core")
        give_ref[...] = projected(hidden, w_out_ref, 1 - core, planes, width)

    whole = pl.BlockSpec(memory_space=pltpu.VMEM)
    return pl.pallas_call(
        kernel,
        out_shape=[
            jax.ShapeDtypeStruct((own, hidden_width), BF16),
            jax.ShapeDtypeStruct((planes, own, width), BF16),
        ],
        in_specs=[whole, whole, whole],
        out_specs=[whole, whole],
        compiler_params=pltpu.CompilerParams(vmem_limit_bytes=LIMIT),
        cost_estimate=pl.CostEstimate(
            flops=4 * own * width * expert * hidden_width * own,
            bytes_accessed=2 * (w_in.size + w_out.size),
            transcendentals=own * hidden_width,
        ),
        name="experts",
    )(
        got,
        pltpu.with_memory_space_constraint(w_in, pltpu.VMEM),
        pltpu.with_memory_space_constraint(w_out, pltpu.VMEM),
    )


def mix(combine, back, seq, planes):
    slots, count = combine.shape
    pair, width = back.shape[1:]
    own = pair // 2
    steps = count // MIX

    def kernel(combine_ref, back_ref, out_ref, held_ref, sems):
        core = lax.axis_index("core")
        parts = []
        for z in range(planes):
            total = jnp.zeros((pair, width), F32)
            for s in range(seq):
                total += back_ref[s * planes + z].astype(F32)
            near, far = total[:own], total[own:]
            parts += [jnp.where(core == 0, near, far), jnp.where(core == 0, far, near)]
        table = jnp.concatenate(parts, axis=0).astype(BF16)
        copies = []
        for step in range(steps):
            rows = pl.ds(step * MIX, MIX)
            held_ref[rows, :] = lax.dot_general(
                combine_ref[:, rows], table, (((0,), (0,)), ((), ())), preferred_element_type=F32
            )
            copy = pltpu.make_async_copy(held_ref.at[rows], out_ref.at[rows], sems.at[step])
            copy.start()
            copies.append(copy)
        for copy in copies:
            copy.wait()

    whole = pl.BlockSpec(memory_space=pltpu.VMEM)
    return pl.pallas_call(
        kernel,
        out_shape=jax.ShapeDtypeStruct((count, width), F32),
        in_specs=[whole, whole],
        out_specs=pl.BlockSpec(memory_space=pltpu.HBM),
        scratch_shapes=[
            pltpu.VMEM((count, width), F32),
            pltpu.SemaphoreType.DMA((steps,)),
        ],
        compiler_params=pltpu.CompilerParams(vmem_limit_bytes=LIMIT),
        cost_estimate=pl.CostEstimate(
            flops=2 * slots * count * width, bytes_accessed=4 * count * width, transcendentals=0
        ),
        name="mix",
    )(combine, back)


def local(tokens, slot_keys, w_in, w_out):
    seq = lax.axis_size("seq")
    planes = lax.axis_size("plane")
    expert = 2 * planes

    theirs, far = scores(tokens, slot_keys, False)
    theirs, tokens = lax.optimization_barrier((theirs, tokens))
    gained = swap(theirs, "core")
    mine, near = scores(tokens, slot_keys, True)
    gained, mine = lax.optimization_barrier((gained, mine))
    mine, sent = encode(mine, gained)
    sent, mine, near, far, w_in, w_out = lax.optimization_barrier(
        (sent, mine, near, far, w_in, w_out)
    )
    code = swap(sent, "plane")
    other = swap(mine, "core")
    near_next, far_next = swap(far, "core"), swap(near, "core")
    w_in, w_out = staged(w_in, w_out)
    code, w_in, w_out = lax.optimization_barrier((code, w_in, w_out))
    codes = (code, swap(code, "core"))
    held = (near, far, near_next, far_next)
    send, combine = weigh((mine, other), codes, held, seq, planes)
    got = lax.all_to_all(send, ("seq", "plane"), 0, 0)
    hidden, give = experts(got, w_in, w_out, seq, expert)
    taken = swap(give, "core")
    back = packed(kept(hidden, w_out, planes), taken, seq)
    back = lax.all_to_all(back, ("seq", "plane"), 0, 0)
    return mix(combine, back, seq, planes)


def solution(mesh):
    clips, seq, expert = mesh.devices.shape
    split = jax.sharding.Mesh(
        mesh.devices.reshape(clips, seq, expert // 2, 2), ("clip", "seq", "plane", "core")
    )
    expert = ("plane", "core")
    return jax.shard_map(
        local,
        mesh=split,
        in_specs=(
            P(("clip", "seq"), expert),
            P(expert, None),
            P(expert, None, "seq"),
            P(expert, "seq", None),
        ),
        out_specs=P(("clip", "seq"), expert),
        check_vma=False,
    )
```

```python
import jax
import jax.numpy as jnp
from jax import lax
from jax.experimental import pallas as pl
from jax.experimental.pallas import tpu as pltpu
from jax.sharding import PartitionSpec as P

BF16 = jnp.bfloat16
F32 = jnp.float32
LANES = 128
REACH = 124.0
BLOCK = 1024
MIX = 512
LIMIT = 16 * 2**20


def swap(value, axis):
    return lax.ppermute(value, axis, [(0, 1), (1, 0)])


def spread(value, lane, first):
    high = value.astype(BF16).astype(F32)
    middle = (value - high).astype(BF16).astype(F32)
    low = value - high - middle
    parts = jnp.where(lane == first, high, 0.0)
    parts = jnp.where(lane == first + 1, middle, parts)
    return jnp.where(lane == first + 2, low, parts)


def call(kernel, name, out_shape, inputs, flops=0, scratch=()):
    whole = pl.BlockSpec(memory_space=pltpu.VMEM)
    moved = sum(a.size * a.dtype.itemsize for a in inputs)
    return pl.pallas_call(
        kernel,
        out_shape=out_shape,
        in_specs=[whole] * len(inputs),
        out_specs=jax.tree.map(lambda _: whole, out_shape),
        scratch_shapes=scratch,
        compiler_params=pltpu.CompilerParams(vmem_limit_bytes=LIMIT),
        cost_estimate=pl.CostEstimate(flops=flops, bytes_accessed=moved, transcendentals=0),
        name=name,
    )(*inputs)


def encode(mine, gained):
    slots, count = mine.shape

    def kernel(mine_ref, gained_ref, total_ref, code_ref):
        total = mine_ref[...] + gained_ref[...]
        total_ref[...] = total
        high = jnp.max(total, axis=1, keepdims=True)
        low = jnp.min(total, axis=1, keepdims=True)
        center = 0.5 * (high + low)
        span = jnp.maximum(high - low, jnp.maximum(jnp.abs(center) * 2.0**-16, 1e-30))
        code = jnp.exp2((total - center) * (2 * REACH / span))
        code_ref[:, :count] = code.astype(BF16)
        lane = lax.broadcasted_iota(jnp.int32, (slots, LANES), 1)
        side = spread(center, lane, 0) + spread(span, lane, 3)
        code_ref[:, count:] = side.astype(BF16)

    return call(
        kernel,
        "encode",
        (
            jax.ShapeDtypeStruct((slots, count), F32),
            jax.ShapeDtypeStruct((slots, count + LANES), BF16),
        ),
        (mine, gained),
    )


def decoded(total, code):
    count = total.shape[1]
    side = code[:, count:].astype(F32)
    lane = lax.broadcasted_iota(jnp.int32, side.shape, 1)
    center = jnp.sum(jnp.where(lane < 3, side, 0.0), axis=1, keepdims=True)
    span = jnp.sum(jnp.where(lane < 3, 0.0, side), axis=1, keepdims=True)
    power = jnp.log2(code[:, :count].astype(F32))
    return total + (power * (span / (2 * REACH)) + center)


def weigh(totals_of, codes, held, seq, planes):
    slots, half = totals_of[0].shape
    width = held[0].shape[1]
    own = slots // planes // 2

    def kernel(mine_ref, other_ref, code_ref, sent_ref, *refs):
        held_ref, next_ref, send_ref, combine_ref = refs
        core = lax.axis_index("core")
        places = [
            pl.ds(pl.multiple_of(start, half), half) for start in (core * half, (1 - core) * half)
        ]
        parts = [decoded(mine_ref[...], code_ref[...]), decoded(other_ref[...], sent_ref[...])]
        first, second = [], []
        for part, place in zip(parts, places):
            shifted = jnp.exp(part - jnp.max(part, axis=0, keepdims=True))
            share = shifted / jnp.sum(shifted, axis=0, keepdims=True)
            combine_ref[:, place] = share.astype(BF16)
            rows = [part[k * own : (k + 1) * own] for k in range(2 * planes)]
            first += [jnp.where(core == 0, rows[2 * z], rows[2 * z + 1]) for z in range(planes)]
        parts = [jnp.concatenate(first[k * planes : (k + 1) * planes], axis=0) for k in range(2)]
        top = jnp.max(jnp.maximum(parts[0], parts[1]), axis=1, keepdims=True)
        dispatch = [jnp.exp(part - top).astype(BF16) for part in parts]
        totals = sum(jnp.sum(d.astype(F32), axis=1, keepdims=True) for d in dispatch)

        def gathered(a, b):
            return (
                jnp.dot(dispatch[0], a, preferred_element_type=F32)
                + jnp.dot(dispatch[1], b, preferred_element_type=F32)
            ) / totals

        near, far = pl.ds(0, half), pl.ds(half, half)
        ours = gathered(held_ref[near], held_ref[far])
        next_ours = gathered(next_ref[far], next_ref[near])
        mean = jnp.concatenate(
            [jnp.where(core == 0, ours, next_ours), jnp.where(core == 0, next_ours, ours)], axis=1
        )
        lane = lax.broadcasted_iota(jnp.int32, (planes * own, LANES), 1)
        weight = top + jnp.log(totals)
        first, second = spread(weight, lane, 0), spread(weight, lane, 3)
        for z in range(planes):
            near_rows = slice(z * own, z * own + own // 2)
            far_rows = slice(z * own + own // 2, (z + 1) * own)
            piece = [mean[near_rows], mean[far_rows], first[near_rows] + second[far_rows]]
            piece = jnp.concatenate(piece, axis=1).astype(BF16)
            for s in range(seq):
                send_ref[s * planes + z] = piece

    return call(
        kernel,
        "weigh",
        (
            jax.ShapeDtypeStruct((seq * planes, own // 2, 4 * width + LANES), BF16),
            jax.ShapeDtypeStruct((slots, 2 * half), BF16),
        ),
        (*totals_of, *codes, *held),
        flops=8 * planes * own * half * width,
    )


def scores(tokens, slot_keys, held=None):
    count, width = tokens.shape
    slots = slot_keys.shape[1]
    half = count // 2
    steps = half // BLOCK
    mine = held is not None

    def kernel(keys_hbm, tokens_ref, *refs):
        part_ref, held_ref, keys_ref, sems = refs[-4:]
        core = lax.axis_index("core")
        start = (core if mine else 1 - core) * half
        copies = []
        for step in range(steps):
            source = pl.ds(pl.multiple_of(start + step * BLOCK, BLOCK), BLOCK)
            target = pl.ds((0 if mine else half) + step * BLOCK, BLOCK)
            copies.append(
                pltpu.make_async_copy(
                    tokens_ref.at[source], held_ref.at[target], sems.at[step]
                )
            )
        keys = pltpu.make_async_copy(keys_hbm, keys_ref, sems.at[steps])
        keys.start()
        for copy in copies:
            copy.start()
        keys.wait()
        for step in range(steps):
            copies[step].wait()
            part_ref[:, pl.ds(step * BLOCK, BLOCK)] = lax.dot_general(
                keys_ref[...],
                held_ref[pl.ds((0 if mine else half) + step * BLOCK, BLOCK)],
                (((1,), (1,)), ((), ())),
                preferred_element_type=F32,
            )

    whole = pl.BlockSpec(memory_space=pltpu.VMEM)
    return pl.pallas_call(
        kernel,
        out_shape=(
            jax.ShapeDtypeStruct((slots, half), F32),
            pltpu.VMEM((count, width), BF16),
        ),
        in_specs=[pl.BlockSpec(memory_space=pltpu.HBM)] * 2 + [whole] * mine,
        input_output_aliases={2: 1} if mine else {},
        out_specs=(whole, whole),
        scratch_shapes=[
            pltpu.VMEM((slots, width), BF16),
            pltpu.SemaphoreType.DMA((steps + 1,)),
        ],
        compiler_params=pltpu.CompilerParams(vmem_limit_bytes=LIMIT),
        cost_estimate=pl.CostEstimate(
            flops=2 * slots * half * width, bytes_accessed=4 * half * width, transcendentals=0
        ),
        name="scores_mine" if mine else "scores_theirs",
    )(
        pltpu.with_memory_space_constraint(slot_keys.T, pltpu.HBM),
        pltpu.with_memory_space_constraint(tokens, pltpu.HBM),
        *([held] if mine else []),
    )


def staged(first, second):
    pieces = first.shape[0]

    def kernel(first_ref, second_ref, first_out, second_out, sems):
        copies = []
        for i in range(pieces):
            copies.append(
                pltpu.make_async_copy(first_ref.at[i], first_out.at[i], sems.at[0, i])
            )
            copies.append(
                pltpu.make_async_copy(second_ref.at[i], second_out.at[i], sems.at[1, i])
            )
        for item in copies:
            item.start()
        for item in copies:
            item.wait()

    outside = pl.BlockSpec(memory_space=pltpu.HBM)
    whole = pl.BlockSpec(memory_space=pltpu.VMEM)
    return pl.pallas_call(
        kernel,
        out_shape=(pltpu.VMEM(first.shape, first.dtype), pltpu.VMEM(second.shape, second.dtype)),
        in_specs=[outside, outside],
        out_specs=(whole, whole),
        scratch_shapes=[pltpu.SemaphoreType.DMA((2, pieces))],
        compiler_params=pltpu.CompilerParams(vmem_limit_bytes=LIMIT),
        cost_estimate=pl.CostEstimate(
            flops=0, bytes_accessed=4 * (first.size + second.size), transcendentals=0
        ),
        name="staged",
    )(
        pltpu.with_memory_space_constraint(first, pltpu.HBM),
        pltpu.with_memory_space_constraint(second, pltpu.HBM),
    )


def projected(hidden, w_out_ref, core, planes, width):
    own = hidden.shape[0]
    rows = lax.broadcasted_iota(jnp.int32, (own, width), 0)
    results = []
    for z in range(planes):
        start = pl.multiple_of((2 * z + core) * width, width)
        result = jnp.zeros((own, width), F32)
        for i in range(own):
            part = jnp.dot(
                hidden, w_out_ref[i, :, pl.ds(start, width)], preferred_element_type=F32
            )
            result = jnp.where(rows == i, part, result)
        results.append(result.astype(BF16))
    return jnp.stack(results)


def kept(hidden, w_out, planes):
    own, width = w_out.shape[0], w_out.shape[2] // planes // 2

    def kernel(hidden_ref, w_out_ref, out_ref):
        core = lax.axis_index("core")
        out_ref[...] = projected(hidden_ref[...], w_out_ref, core, planes, width)

    return call(
        kernel,
        "kept",
        jax.ShapeDtypeStruct((planes, own, width), BF16),
        (hidden, pltpu.with_memory_space_constraint(w_out, pltpu.VMEM)),
        flops=16 * w_out.size,
    )


def packed(keep, taken, seq):
    planes, own, width = keep.shape

    def kernel(keep_ref, taken_ref, out_ref):
        for z in range(planes):
            pair = jnp.concatenate([keep_ref[z], taken_ref[z]], axis=0)
            for s in range(seq):
                out_ref[s * planes + z] = pair

    return call(
        kernel,
        "packed",
        jax.ShapeDtypeStruct((seq * planes, 2 * own, width), BF16),
        (keep, taken),
    )


def experts(got, w_in, w_out, seq, expert):
    own, width = w_in.shape[0], w_in.shape[1] // expert
    planes = expert // 2
    hidden_width = w_in.shape[2]

    def kernel(got_ref, w_in_ref, w_out_ref, hidden_ref, give_ref):
        side = got_ref[:, :, 4 * width :].astype(F32)
        lane = lax.broadcasted_iota(jnp.int32, side.shape, 2)
        scales = []
        for wanted in (lane < 3, lane >= 3):
            weight = jnp.sum(jnp.where(wanted, side, 0.0), axis=-1, keepdims=True)
            weight = weight.reshape(seq, planes, own // 2, 1)
            scale = jnp.exp(weight - jnp.max(weight, axis=0, keepdims=True))
            scales.append(scale / jnp.sum(scale, axis=0, keepdims=True))
        pieces = []
        for z in range(planes):
            halves = []
            for k in range(2):
                total = jnp.zeros((own // 2, 2 * width), F32)
                for s in range(seq):
                    part = got_ref[s * planes + z, :, 2 * k * width : 2 * (k + 1) * width]
                    total += part.astype(F32) * scales[k][s, z]
                halves.append(total)
            both = jnp.concatenate(halves, axis=0).astype(BF16)
            pieces += [both[:, :width], both[:, width:]]
        rows = lax.broadcasted_iota(jnp.int32, (own, hidden_width), 0)
        inner = jnp.zeros((own, hidden_width), F32)
        for i in range(own):
            total = jnp.zeros((own, hidden_width), F32)
            for e in range(expert):
                total += jnp.dot(
                    pieces[e],
                    w_in_ref[i, e * width : (e + 1) * width, :],
                    preferred_element_type=F32,
                )
            inner = jnp.where(rows == i, total, inner)
        hidden = 0.5 * inner * (1.0 + lax.erf(inner * (0.5**0.5)))
        hidden = hidden.astype(BF16)
        hidden_ref[...] = hidden
        core = lax.axis_index("core")
        give_ref[...] = projected(hidden, w_out_ref, 1 - core, planes, width)

    whole = pl.BlockSpec(memory_space=pltpu.VMEM)
    return pl.pallas_call(
        kernel,
        out_shape=[
            jax.ShapeDtypeStruct((own, hidden_width), BF16),
            jax.ShapeDtypeStruct((planes, own, width), BF16),
        ],
        in_specs=[whole, whole, whole],
        out_specs=[whole, whole],
        compiler_params=pltpu.CompilerParams(vmem_limit_bytes=LIMIT),
        cost_estimate=pl.CostEstimate(
            flops=4 * own * width * expert * hidden_width * own,
            bytes_accessed=2 * (w_in.size + w_out.size),
            transcendentals=own * hidden_width,
        ),
        name="experts",
    )(
        got,
        pltpu.with_memory_space_constraint(w_in, pltpu.VMEM),
        pltpu.with_memory_space_constraint(w_out, pltpu.VMEM),
    )


def mix(combine, back, seq, planes):
    slots, count = combine.shape
    pair, width = back.shape[1:]
    own = pair // 2
    steps = count // MIX

    def kernel(combine_ref, back_ref, out_ref, held_ref, sems):
        core = lax.axis_index("core")
        parts = []
        for z in range(planes):
            total = jnp.zeros((pair, width), F32)
            for s in range(seq):
                total += back_ref[s * planes + z].astype(F32)
            near, far = total[:own], total[own:]
            parts += [jnp.where(core == 0, near, far), jnp.where(core == 0, far, near)]
        table = jnp.concatenate(parts, axis=0).astype(BF16)
        copies = []
        for step in range(steps):
            rows = pl.ds(step * MIX, MIX)
            held_ref[rows, :] = lax.dot_general(
                combine_ref[:, rows], table, (((0,), (0,)), ((), ())), preferred_element_type=F32
            )
            copy = pltpu.make_async_copy(held_ref.at[rows], out_ref.at[rows], sems.at[step])
            copy.start()
            copies.append(copy)
        for copy in copies:
            copy.wait()

    whole = pl.BlockSpec(memory_space=pltpu.VMEM)
    return pl.pallas_call(
        kernel,
        out_shape=jax.ShapeDtypeStruct((count, width), F32),
        in_specs=[whole, whole],
        out_specs=pl.BlockSpec(memory_space=pltpu.HBM),
        scratch_shapes=[
            pltpu.VMEM((count, width), F32),
            pltpu.SemaphoreType.DMA((steps,)),
        ],
        compiler_params=pltpu.CompilerParams(vmem_limit_bytes=LIMIT),
        cost_estimate=pl.CostEstimate(
            flops=2 * slots * count * width, bytes_accessed=4 * count * width, transcendentals=0
        ),
        name="mix",
    )(combine, back)


def local(tokens, slot_keys, w_in, w_out):
    seq = lax.axis_size("seq")
    planes = lax.axis_size("plane")
    expert = 2 * planes

    theirs, held = scores(tokens, slot_keys)
    theirs, tokens = lax.optimization_barrier((theirs, tokens))
    gained = swap(theirs, "core")
    mine, held = scores(tokens, slot_keys, held)
    gained, mine = lax.optimization_barrier((gained, mine))
    mine, sent = encode(mine, gained)
    sent, mine, held, w_in, w_out = lax.optimization_barrier((sent, mine, held, w_in, w_out))
    code = swap(sent, "plane")
    other = swap(mine, "core")
    held = (held, swap(held, "core"))
    w_in, w_out = staged(w_in, w_out)
    code, w_in, w_out = lax.optimization_barrier((code, w_in, w_out))
    codes = (code, swap(code, "core"))
    send, combine = weigh((mine, other), codes, held, seq, planes)
    got = lax.all_to_all(send, ("seq", "plane"), 0, 0)
    hidden, give = experts(got, w_in, w_out, seq, expert)
    taken = swap(give, "core")
    back = packed(kept(hidden, w_out, planes), taken, seq)
    back = lax.all_to_all(back, ("seq", "plane"), 0, 0)
    return mix(combine, back, seq, planes)


def solution(mesh):
    clips, seq, expert = mesh.devices.shape
    split = jax.sharding.Mesh(
        mesh.devices.reshape(clips, seq, expert // 2, 2), ("clip", "seq", "plane", "core")
    )
    expert = ("plane", "core")
    return jax.shard_map(
        local,
        mesh=split,
        in_specs=(
            P(("clip", "seq"), expert),
            P(expert, None),
            P(expert, None, "seq"),
            P(expert, "seq", None),
        ),
        out_specs=P(("clip", "seq"), expert),
        check_vma=False,
    )
```

```python
import jax
import jax.numpy as jnp
from jax import lax
from jax.experimental import pallas as pl
from jax.experimental.pallas import tpu as pltpu
from jax.sharding import PartitionSpec as P

BF16 = jnp.bfloat16
F32 = jnp.float32
LANES = 128
REACH = 124.0
BLOCK = 1024
MIX = 512
LIMIT = 16 * 2**20


def swap(value, axis):
    return lax.ppermute(value, axis, [(0, 1), (1, 0)])


def spread(value, lane, first):
    high = value.astype(BF16).astype(F32)
    middle = (value - high).astype(BF16).astype(F32)
    low = value - high - middle
    parts = jnp.where(lane == first, high, 0.0)
    parts = jnp.where(lane == first + 1, middle, parts)
    return jnp.where(lane == first + 2, low, parts)


def call(kernel, name, out_shape, inputs, flops=0, scratch=()):
    whole = pl.BlockSpec(memory_space=pltpu.VMEM)
    moved = sum(a.size * a.dtype.itemsize for a in inputs)
    return pl.pallas_call(
        kernel,
        out_shape=out_shape,
        in_specs=[whole] * len(inputs),
        out_specs=jax.tree.map(lambda _: whole, out_shape),
        scratch_shapes=scratch,
        compiler_params=pltpu.CompilerParams(vmem_limit_bytes=LIMIT),
        cost_estimate=pl.CostEstimate(flops=flops, bytes_accessed=moved, transcendentals=0),
        name=name,
    )(*inputs)


def encode(mine, gained):
    slots, count = mine.shape

    def kernel(mine_ref, gained_ref, total_ref, code_ref):
        total = mine_ref[...] + gained_ref[...]
        total_ref[...] = total
        high = jnp.max(total, axis=1, keepdims=True)
        low = jnp.min(total, axis=1, keepdims=True)
        center = 0.5 * (high + low)
        span = jnp.maximum(high - low, jnp.maximum(jnp.abs(center) * 2.0**-16, 1e-30))
        code = jnp.exp2((total - center) * (2 * REACH / span))
        code_ref[:, :count] = code.astype(BF16)
        lane = lax.broadcasted_iota(jnp.int32, (slots, LANES), 1)
        side = spread(center, lane, 0) + spread(span, lane, 3)
        code_ref[:, count:] = side.astype(BF16)

    return call(
        kernel,
        "encode",
        (
            jax.ShapeDtypeStruct((slots, count), F32),
            jax.ShapeDtypeStruct((slots, count + LANES), BF16),
        ),
        (mine, gained),
    )


def decoded(total, code):
    count = total.shape[1]
    side = code[:, count:].astype(F32)
    lane = lax.broadcasted_iota(jnp.int32, side.shape, 1)
    center = jnp.sum(jnp.where(lane < 3, side, 0.0), axis=1, keepdims=True)
    span = jnp.sum(jnp.where(lane < 3, 0.0, side), axis=1, keepdims=True)
    power = jnp.log2(code[:, :count].astype(F32))
    return total + (power * (span / (2 * REACH)) + center)


def weigh(totals_of, codes, held, seq, planes):
    slots, half = totals_of[0].shape
    width = held[0].shape[1]
    own = slots // planes // 2

    def kernel(mine_ref, other_ref, code_ref, sent_ref, *refs):
        held_ref, next_ref, send_ref, logits_ref = refs
        core = lax.axis_index("core")
        places = [
            pl.ds(pl.multiple_of(start, half), half) for start in (core * half, (1 - core) * half)
        ]
        parts = [decoded(mine_ref[...], code_ref[...]), decoded(other_ref[...], sent_ref[...])]
        first, second = [], []
        for part, place in zip(parts, places):
            logits_ref[:, place] = part
            rows = [part[k * own : (k + 1) * own] for k in range(2 * planes)]
            first += [jnp.where(core == 0, rows[2 * z], rows[2 * z + 1]) for z in range(planes)]
        parts = [jnp.concatenate(first[k * planes : (k + 1) * planes], axis=0) for k in range(2)]
        top = jnp.max(jnp.maximum(parts[0], parts[1]), axis=1, keepdims=True)
        dispatch = [jnp.exp(part - top).astype(BF16) for part in parts]
        totals = sum(jnp.sum(d.astype(F32), axis=1, keepdims=True) for d in dispatch)

        def gathered(a, b):
            return (
                jnp.dot(dispatch[0], a, preferred_element_type=F32)
                + jnp.dot(dispatch[1], b, preferred_element_type=F32)
            ) / totals

        near, far = pl.ds(0, half), pl.ds(half, half)
        ours = gathered(held_ref[near], held_ref[far])
        next_ours = gathered(next_ref[far], next_ref[near])
        mean = jnp.concatenate(
            [jnp.where(core == 0, ours, next_ours), jnp.where(core == 0, next_ours, ours)], axis=1
        )
        lane = lax.broadcasted_iota(jnp.int32, (planes * own, LANES), 1)
        weight = top + jnp.log(totals)
        first, second = spread(weight, lane, 0), spread(weight, lane, 3)
        for z in range(planes):
            near_rows = slice(z * own, z * own + own // 2)
            far_rows = slice(z * own + own // 2, (z + 1) * own)
            piece = [mean[near_rows], mean[far_rows], first[near_rows] + second[far_rows]]
            piece = jnp.concatenate(piece, axis=1).astype(BF16)
            for s in range(seq):
                send_ref[s * planes + z] = piece

    return call(
        kernel,
        "weigh",
        (
            jax.ShapeDtypeStruct((seq * planes, own // 2, 4 * width + LANES), BF16),
            jax.ShapeDtypeStruct((slots, 2 * half), F32),
        ),
        (*totals_of, *codes, *held),
        flops=8 * planes * own * half * width,
    )


def scores(tokens, slot_keys, held=None):
    count, width = tokens.shape
    slots = slot_keys.shape[1]
    half = count // 2
    steps = half // BLOCK
    mine = held is not None

    def kernel(keys_hbm, tokens_ref, *refs):
        part_ref, held_ref, keys_ref, sems = refs[-4:]
        core = lax.axis_index("core")
        start = (core if mine else 1 - core) * half
        copies = []
        for step in range(steps):
            source = pl.ds(pl.multiple_of(start + step * BLOCK, BLOCK), BLOCK)
            target = pl.ds((0 if mine else half) + step * BLOCK, BLOCK)
            copies.append(
                pltpu.make_async_copy(
                    tokens_ref.at[source], held_ref.at[target], sems.at[step]
                )
            )
        keys = pltpu.make_async_copy(keys_hbm, keys_ref, sems.at[steps])
        keys.start()
        for copy in copies:
            copy.start()
        keys.wait()
        for step in range(steps):
            copies[step].wait()
            part_ref[:, pl.ds(step * BLOCK, BLOCK)] = lax.dot_general(
                keys_ref[...],
                held_ref[pl.ds((0 if mine else half) + step * BLOCK, BLOCK)],
                (((1,), (1,)), ((), ())),
                preferred_element_type=F32,
            )

    whole = pl.BlockSpec(memory_space=pltpu.VMEM)
    return pl.pallas_call(
        kernel,
        out_shape=(
            jax.ShapeDtypeStruct((slots, half), F32),
            pltpu.VMEM((count, width), BF16),
        ),
        in_specs=[pl.BlockSpec(memory_space=pltpu.HBM)] * 2 + [whole] * mine,
        input_output_aliases={2: 1} if mine else {},
        out_specs=(whole, whole),
        scratch_shapes=[
            pltpu.VMEM((slots, width), BF16),
            pltpu.SemaphoreType.DMA((steps + 1,)),
        ],
        compiler_params=pltpu.CompilerParams(vmem_limit_bytes=LIMIT),
        cost_estimate=pl.CostEstimate(
            flops=2 * slots * half * width, bytes_accessed=4 * half * width, transcendentals=0
        ),
        name="scores_mine" if mine else "scores_theirs",
    )(
        pltpu.with_memory_space_constraint(slot_keys.T, pltpu.HBM),
        pltpu.with_memory_space_constraint(tokens, pltpu.HBM),
        *([held] if mine else []),
    )


def staged(first, second):
    pieces = first.shape[0]

    def kernel(first_ref, second_ref, first_out, second_out, sems):
        copies = []
        for i in range(pieces):
            copies.append(
                pltpu.make_async_copy(first_ref.at[i], first_out.at[i], sems.at[0, i])
            )
            copies.append(
                pltpu.make_async_copy(second_ref.at[i], second_out.at[i], sems.at[1, i])
            )
        for item in copies:
            item.start()
        for item in copies:
            item.wait()

    outside = pl.BlockSpec(memory_space=pltpu.HBM)
    whole = pl.BlockSpec(memory_space=pltpu.VMEM)
    return pl.pallas_call(
        kernel,
        out_shape=(pltpu.VMEM(first.shape, first.dtype), pltpu.VMEM(second.shape, second.dtype)),
        in_specs=[outside, outside],
        out_specs=(whole, whole),
        scratch_shapes=[pltpu.SemaphoreType.DMA((2, pieces))],
        compiler_params=pltpu.CompilerParams(vmem_limit_bytes=LIMIT),
        cost_estimate=pl.CostEstimate(
            flops=0, bytes_accessed=4 * (first.size + second.size), transcendentals=0
        ),
        name="staged",
    )(
        pltpu.with_memory_space_constraint(first, pltpu.HBM),
        pltpu.with_memory_space_constraint(second, pltpu.HBM),
    )


def projected(hidden, w_out_ref, core, planes, width):
    own = hidden.shape[0]
    rows = lax.broadcasted_iota(jnp.int32, (own, width), 0)
    results = []
    for z in range(planes):
        start = pl.multiple_of((2 * z + core) * width, width)
        result = jnp.zeros((own, width), F32)
        for i in range(own):
            part = jnp.dot(
                hidden, w_out_ref[i, :, pl.ds(start, width)], preferred_element_type=F32
            )
            result = jnp.where(rows == i, part, result)
        results.append(result.astype(BF16))
    return jnp.stack(results)


def kept(hidden, w_out, logits, planes):
    own, width = w_out.shape[0], w_out.shape[2] // planes // 2
    slots, count = logits.shape

    def kernel(hidden_ref, w_out_ref, logits_ref, out_ref, combine_ref):
        core = lax.axis_index("core")
        out_ref[...] = projected(hidden_ref[...], w_out_ref, core, planes, width)
        for start in range(0, count, BLOCK):
            part = logits_ref[:, start : start + BLOCK]
            shifted = jnp.exp(part - jnp.max(part, axis=0, keepdims=True))
            share = shifted / jnp.sum(shifted, axis=0, keepdims=True)
            combine_ref[:, start : start + BLOCK] = share.astype(BF16)

    return call(
        kernel,
        "kept",
        (
            jax.ShapeDtypeStruct((planes, own, width), BF16),
            jax.ShapeDtypeStruct((slots, count), BF16),
        ),
        (hidden, pltpu.with_memory_space_constraint(w_out, pltpu.VMEM), logits),
        flops=16 * w_out.size,
    )


def packed(keep, taken, seq):
    planes, own, width = keep.shape

    def kernel(keep_ref, taken_ref, out_ref):
        for z in range(planes):
            pair = jnp.concatenate([keep_ref[z], taken_ref[z]], axis=0)
            for s in range(seq):
                out_ref[s * planes + z] = pair

    return call(
        kernel,
        "packed",
        jax.ShapeDtypeStruct((seq * planes, 2 * own, width), BF16),
        (keep, taken),
    )


def experts(got, w_in, w_out, seq, expert):
    own, width = w_in.shape[0], w_in.shape[1] // expert
    planes = expert // 2
    hidden_width = w_in.shape[2]

    def kernel(got_ref, w_in_ref, w_out_ref, hidden_ref, give_ref):
        side = got_ref[:, :, 4 * width :].astype(F32)
        lane = lax.broadcasted_iota(jnp.int32, side.shape, 2)
        scales = []
        for wanted in (lane < 3, lane >= 3):
            weight = jnp.sum(jnp.where(wanted, side, 0.0), axis=-1, keepdims=True)
            weight = weight.reshape(seq, planes, own // 2, 1)
            scale = jnp.exp(weight - jnp.max(weight, axis=0, keepdims=True))
            scales.append(scale / jnp.sum(scale, axis=0, keepdims=True))
        pieces = []
        for z in range(planes):
            halves = []
            for k in range(2):
                total = jnp.zeros((own // 2, 2 * width), F32)
                for s in range(seq):
                    part = got_ref[s * planes + z, :, 2 * k * width : 2 * (k + 1) * width]
                    total += part.astype(F32) * scales[k][s, z]
                halves.append(total)
            both = jnp.concatenate(halves, axis=0).astype(BF16)
            pieces += [both[:, :width], both[:, width:]]
        rows = lax.broadcasted_iota(jnp.int32, (own, hidden_width), 0)
        inner = jnp.zeros((own, hidden_width), F32)
        for i in range(own):
            total = jnp.zeros((own, hidden_width), F32)
            for e in range(expert):
                total += jnp.dot(
                    pieces[e],
                    w_in_ref[i, e * width : (e + 1) * width, :],
                    preferred_element_type=F32,
                )
            inner = jnp.where(rows == i, total, inner)
        hidden = 0.5 * inner * (1.0 + lax.erf(inner * (0.5**0.5)))
        hidden = hidden.astype(BF16)
        hidden_ref[...] = hidden
        core = lax.axis_index("core")
        give_ref[...] = projected(hidden, w_out_ref, 1 - core, planes, width)

    whole = pl.BlockSpec(memory_space=pltpu.VMEM)
    return pl.pallas_call(
        kernel,
        out_shape=[
            jax.ShapeDtypeStruct((own, hidden_width), BF16),
            jax.ShapeDtypeStruct((planes, own, width), BF16),
        ],
        in_specs=[whole, whole, whole],
        out_specs=[whole, whole],
        compiler_params=pltpu.CompilerParams(vmem_limit_bytes=LIMIT),
        cost_estimate=pl.CostEstimate(
            flops=4 * own * width * expert * hidden_width * own,
            bytes_accessed=2 * (w_in.size + w_out.size),
            transcendentals=own * hidden_width,
        ),
        name="experts",
    )(
        got,
        pltpu.with_memory_space_constraint(w_in, pltpu.VMEM),
        pltpu.with_memory_space_constraint(w_out, pltpu.VMEM),
    )


def mix(combine, back, seq, planes):
    slots, count = combine.shape
    pair, width = back.shape[1:]
    own = pair // 2
    steps = count // MIX

    def kernel(combine_ref, back_ref, out_ref, held_ref, sems):
        core = lax.axis_index("core")
        parts = []
        for z in range(planes):
            total = jnp.zeros((pair, width), F32)
            for s in range(seq):
                total += back_ref[s * planes + z].astype(F32)
            near, far = total[:own], total[own:]
            parts += [jnp.where(core == 0, near, far), jnp.where(core == 0, far, near)]
        table = jnp.concatenate(parts, axis=0).astype(BF16)
        copies = []
        for step in range(steps):
            rows = pl.ds(step * MIX, MIX)
            held_ref[rows, :] = lax.dot_general(
                combine_ref[:, rows], table, (((0,), (0,)), ((), ())), preferred_element_type=F32
            )
            copy = pltpu.make_async_copy(held_ref.at[rows], out_ref.at[rows], sems.at[step])
            copy.start()
            copies.append(copy)
        for copy in copies:
            copy.wait()

    whole = pl.BlockSpec(memory_space=pltpu.VMEM)
    return pl.pallas_call(
        kernel,
        out_shape=jax.ShapeDtypeStruct((count, width), F32),
        in_specs=[whole, whole],
        out_specs=pl.BlockSpec(memory_space=pltpu.HBM),
        scratch_shapes=[
            pltpu.VMEM((count, width), F32),
            pltpu.SemaphoreType.DMA((steps,)),
        ],
        compiler_params=pltpu.CompilerParams(vmem_limit_bytes=LIMIT),
        cost_estimate=pl.CostEstimate(
            flops=2 * slots * count * width, bytes_accessed=4 * count * width, transcendentals=0
        ),
        name="mix",
    )(combine, back)


def local(tokens, slot_keys, w_in, w_out):
    seq = lax.axis_size("seq")
    planes = lax.axis_size("plane")
    expert = 2 * planes

    theirs, held = scores(tokens, slot_keys)
    theirs, tokens = lax.optimization_barrier((theirs, tokens))
    gained = swap(theirs, "core")
    mine, held = scores(tokens, slot_keys, held)
    gained, mine = lax.optimization_barrier((gained, mine))
    mine, sent = encode(mine, gained)
    sent, mine, held, w_in, w_out = lax.optimization_barrier((sent, mine, held, w_in, w_out))
    code = swap(sent, "plane")
    other = swap(mine, "core")
    held = (held, swap(held, "core"))
    w_in, w_out = staged(w_in, w_out)
    code, w_in, w_out = lax.optimization_barrier((code, w_in, w_out))
    codes = (code, swap(code, "core"))
    send, logits = weigh((mine, other), codes, held, seq, planes)
    got = lax.all_to_all(send, ("seq", "plane"), 0, 0)
    hidden, give = experts(got, w_in, w_out, seq, expert)
    taken = swap(give, "core")
    keep, combine = kept(hidden, w_out, logits, planes)
    back = packed(keep, taken, seq)
    back = lax.all_to_all(back, ("seq", "plane"), 0, 0)
    return mix(combine, back, seq, planes)


def solution(mesh):
    clips, seq, expert = mesh.devices.shape
    split = jax.sharding.Mesh(
        mesh.devices.reshape(clips, seq, expert // 2, 2), ("clip", "seq", "plane", "core")
    )
    expert = ("plane", "core")
    return jax.shard_map(
        local,
        mesh=split,
        in_specs=(
            P(("clip", "seq"), expert),
            P(expert, None),
            P(expert, None, "seq"),
            P(expert, "seq", None),
        ),
        out_specs=P(("clip", "seq"), expert),
        check_vma=False,
    )
```

```python
import jax
import jax.numpy as jnp
from jax import lax
from jax.experimental import pallas as pl
from jax.experimental.pallas import tpu as pltpu
from jax.sharding import PartitionSpec as P

BF16 = jnp.bfloat16
F32 = jnp.float32
LANES = 128
REACH = 124.0
BLOCK = 1024
MIX = 512
LIMIT = 16 * 2**20


def swap(value, axis):
    return lax.ppermute(value, axis, [(0, 1), (1, 0)])


def spread(value, lane, first):
    high = value.astype(BF16).astype(F32)
    middle = (value - high).astype(BF16).astype(F32)
    low = value - high - middle
    parts = jnp.where(lane == first, high, 0.0)
    parts = jnp.where(lane == first + 1, middle, parts)
    return jnp.where(lane == first + 2, low, parts)


def call(kernel, name, out_shape, inputs, flops=0, scratch=()):
    whole = pl.BlockSpec(memory_space=pltpu.VMEM)
    moved = sum(a.size * a.dtype.itemsize for a in inputs)
    return pl.pallas_call(
        kernel,
        out_shape=out_shape,
        in_specs=[whole] * len(inputs),
        out_specs=jax.tree.map(lambda _: whole, out_shape),
        scratch_shapes=scratch,
        compiler_params=pltpu.CompilerParams(vmem_limit_bytes=LIMIT),
        cost_estimate=pl.CostEstimate(flops=flops, bytes_accessed=moved, transcendentals=0),
        name=name,
    )(*inputs)


def encode(mine, gained):
    slots, count = mine.shape

    def kernel(mine_ref, gained_ref, total_ref, code_ref):
        total = mine_ref[...] + gained_ref[...]
        total_ref[...] = total
        high = jnp.max(total, axis=1, keepdims=True)
        low = jnp.min(total, axis=1, keepdims=True)
        center = 0.5 * (high + low)
        span = jnp.maximum(high - low, jnp.maximum(jnp.abs(center) * 2.0**-16, 1e-30))
        code = jnp.exp2((total - center) * (2 * REACH / span))
        code_ref[:, :count] = code.astype(BF16)
        lane = lax.broadcasted_iota(jnp.int32, (slots, LANES), 1)
        side = spread(center, lane, 0) + spread(span, lane, 3)
        code_ref[:, count:] = side.astype(BF16)

    return call(
        kernel,
        "encode",
        (
            jax.ShapeDtypeStruct((slots, count), F32),
            jax.ShapeDtypeStruct((slots, count + LANES), BF16),
        ),
        (mine, gained),
    )


def decoded(total, code):
    count = total.shape[1]
    side = code[:, count:].astype(F32)
    lane = lax.broadcasted_iota(jnp.int32, side.shape, 1)
    center = jnp.sum(jnp.where(lane < 3, side, 0.0), axis=1, keepdims=True)
    span = jnp.sum(jnp.where(lane < 3, 0.0, side), axis=1, keepdims=True)
    power = jnp.log2(code[:, :count].astype(F32))
    return total + (power * (span / (2 * REACH)) + center)


def weigh(totals_of, codes, held, seq, planes):
    slots, half = totals_of[0].shape
    width = held[0].shape[1]
    own = slots // planes // 2

    def kernel(mine_ref, other_ref, code_ref, sent_ref, *refs):
        held_ref, next_ref, send_ref, logits_ref = refs
        core = lax.axis_index("core")
        places = [
            pl.ds(pl.multiple_of(start, half), half) for start in (core * half, (1 - core) * half)
        ]
        parts = [decoded(mine_ref[...], code_ref[...]), decoded(other_ref[...], sent_ref[...])]
        first, second = [], []
        for part, place in zip(parts, places):
            logits_ref[:, place] = part
            rows = [part[k * own : (k + 1) * own] for k in range(2 * planes)]
            first += [jnp.where(core == 0, rows[2 * z], rows[2 * z + 1]) for z in range(planes)]
        parts = [jnp.concatenate(first[k * planes : (k + 1) * planes], axis=0) for k in range(2)]
        top = jnp.max(jnp.maximum(parts[0], parts[1]), axis=1, keepdims=True)
        dispatch = [jnp.exp(part - top).astype(BF16) for part in parts]
        totals = sum(jnp.sum(d.astype(F32), axis=1, keepdims=True) for d in dispatch)

        def gathered(a, b):
            return (
                jnp.dot(dispatch[0], a, preferred_element_type=F32)
                + jnp.dot(dispatch[1], b, preferred_element_type=F32)
            ) / totals

        near, far = pl.ds(0, half), pl.ds(half, half)
        ours = gathered(held_ref[near], held_ref[far])
        next_ours = gathered(next_ref[far], next_ref[near])
        mean = jnp.concatenate(
            [jnp.where(core == 0, ours, next_ours), jnp.where(core == 0, next_ours, ours)], axis=1
        )
        lane = lax.broadcasted_iota(jnp.int32, (planes * own, LANES), 1)
        weight = top + jnp.log(totals)
        first, second = spread(weight, lane, 0), spread(weight, lane, 3)
        for z in range(planes):
            near_rows = slice(z * own, z * own + own // 2)
            far_rows = slice(z * own + own // 2, (z + 1) * own)
            piece = [mean[near_rows], mean[far_rows], first[near_rows] + second[far_rows]]
            piece = jnp.concatenate(piece, axis=1).astype(BF16)
            for s in range(seq):
                send_ref[s * planes + z] = piece

    return call(
        kernel,
        "weigh",
        (
            jax.ShapeDtypeStruct((seq * planes, own // 2, 4 * width + LANES), BF16),
            jax.ShapeDtypeStruct((slots, 2 * half), F32),
        ),
        (*totals_of, *codes, *held),
        flops=8 * planes * own * half * width,
    )


def scores(tokens, slot_keys, held=None):
    count, width = tokens.shape
    slots = slot_keys.shape[1]
    half = count // 2
    steps = half // BLOCK
    mine = held is not None

    def kernel(keys_hbm, tokens_ref, *refs):
        part_ref, held_ref, keys_ref, sems = refs[-4:]
        core = lax.axis_index("core")
        start = (core if mine else 1 - core) * half
        copies = []
        for step in range(steps):
            source = pl.ds(pl.multiple_of(start + step * BLOCK, BLOCK), BLOCK)
            target = pl.ds((0 if mine else half) + step * BLOCK, BLOCK)
            copies.append(
                pltpu.make_async_copy(
                    tokens_ref.at[source], held_ref.at[target], sems.at[step]
                )
            )
        keys = pltpu.make_async_copy(keys_hbm, keys_ref, sems.at[steps])
        keys.start()
        for copy in copies:
            copy.start()
        keys.wait()
        for step in range(steps):
            copies[step].wait()
            part_ref[:, pl.ds(step * BLOCK, BLOCK)] = lax.dot_general(
                keys_ref[...],
                held_ref[pl.ds((0 if mine else half) + step * BLOCK, BLOCK)],
                (((1,), (1,)), ((), ())),
                preferred_element_type=F32,
            )

    whole = pl.BlockSpec(memory_space=pltpu.VMEM)
    return pl.pallas_call(
        kernel,
        out_shape=(
            jax.ShapeDtypeStruct((slots, half), F32),
            pltpu.VMEM((count, width), BF16),
        ),
        in_specs=[pl.BlockSpec(memory_space=pltpu.HBM)] * 2 + [whole] * mine,
        input_output_aliases={2: 1} if mine else {},
        out_specs=(whole, whole),
        scratch_shapes=[
            pltpu.VMEM((slots, width), BF16),
            pltpu.SemaphoreType.DMA((steps + 1,)),
        ],
        compiler_params=pltpu.CompilerParams(vmem_limit_bytes=LIMIT),
        cost_estimate=pl.CostEstimate(
            flops=2 * slots * half * width, bytes_accessed=4 * half * width, transcendentals=0
        ),
        name="scores_mine" if mine else "scores_theirs",
    )(
        pltpu.with_memory_space_constraint(slot_keys.T, pltpu.HBM),
        pltpu.with_memory_space_constraint(tokens, pltpu.HBM),
        *([held] if mine else []),
    )


def staged(first, second):
    pieces = first.shape[0]

    def kernel(first_ref, second_ref, first_out, second_out, sems):
        copies = []
        for i in range(pieces):
            copies.append(
                pltpu.make_async_copy(first_ref.at[i], first_out.at[i], sems.at[0, i])
            )
            copies.append(
                pltpu.make_async_copy(second_ref.at[i], second_out.at[i], sems.at[1, i])
            )
        for item in copies:
            item.start()
        for item in copies:
            item.wait()

    outside = pl.BlockSpec(memory_space=pltpu.HBM)
    whole = pl.BlockSpec(memory_space=pltpu.VMEM)
    return pl.pallas_call(
        kernel,
        out_shape=(pltpu.VMEM(first.shape, first.dtype), pltpu.VMEM(second.shape, second.dtype)),
        in_specs=[outside, outside],
        out_specs=(whole, whole),
        scratch_shapes=[pltpu.SemaphoreType.DMA((2, pieces))],
        compiler_params=pltpu.CompilerParams(vmem_limit_bytes=LIMIT),
        cost_estimate=pl.CostEstimate(
            flops=0, bytes_accessed=4 * (first.size + second.size), transcendentals=0
        ),
        name="staged",
    )(
        pltpu.with_memory_space_constraint(first, pltpu.HBM),
        pltpu.with_memory_space_constraint(second, pltpu.HBM),
    )


def projected(hidden, w_out_ref, core, planes, width):
    own = hidden.shape[0]
    rows = lax.broadcasted_iota(jnp.int32, (own, width), 0)
    results = []
    for z in range(planes):
        start = pl.multiple_of((2 * z + core) * width, width)
        result = jnp.zeros((own, width), F32)
        for i in range(own):
            part = jnp.dot(
                hidden, w_out_ref[i, :, pl.ds(start, width)], preferred_element_type=F32
            )
            result = jnp.where(rows == i, part, result)
        results.append(result.astype(BF16))
    return jnp.stack(results)


def kept(hidden, w_out, logits, planes):
    own, width = w_out.shape[0], w_out.shape[2] // planes // 2
    slots, count = logits.shape

    def kernel(hidden_ref, w_out_ref, logits_ref, out_ref, combine_ref):
        core = lax.axis_index("core")
        out_ref[...] = projected(hidden_ref[...], w_out_ref, core, planes, width)
        for start in range(0, count, BLOCK):
            part = logits_ref[:, start : start + BLOCK]
            shifted = jnp.exp(part - jnp.max(part, axis=0, keepdims=True))
            share = shifted / jnp.sum(shifted, axis=0, keepdims=True)
            combine_ref[:, start : start + BLOCK] = share.astype(BF16)

    return call(
        kernel,
        "kept",
        (
            jax.ShapeDtypeStruct((planes, own, width), BF16),
            jax.ShapeDtypeStruct((slots, count), BF16),
        ),
        (hidden, pltpu.with_memory_space_constraint(w_out, pltpu.VMEM), logits),
        flops=16 * w_out.size,
    )


def packed(keep, taken, seq):
    planes, own, width = keep.shape

    def kernel(keep_ref, taken_ref, out_ref):
        for z in range(planes):
            pair = jnp.concatenate([keep_ref[z], taken_ref[z]], axis=0)
            for s in range(seq):
                out_ref[s * planes + z] = pair

    return call(
        kernel,
        "packed",
        jax.ShapeDtypeStruct((seq * planes, 2 * own, width), BF16),
        (keep, taken),
    )


def experts(got, w_in, w_out, seq, expert):
    own, width = w_in.shape[0], w_in.shape[1] // expert
    planes = expert // 2
    hidden_width = w_in.shape[2]

    def kernel(got_ref, w_in_ref, w_out_ref, hidden_ref, give_ref):
        side = got_ref[:, :, 4 * width :].astype(F32)
        lane = lax.broadcasted_iota(jnp.int32, side.shape, 2)
        scales = []
        for wanted in (lane < 3, lane >= 3):
            weight = jnp.sum(jnp.where(wanted, side, 0.0), axis=-1, keepdims=True)
            weight = weight.reshape(seq, planes, own // 2, 1)
            scale = jnp.exp(weight - jnp.max(weight, axis=0, keepdims=True))
            scales.append(scale / jnp.sum(scale, axis=0, keepdims=True))
        pieces = []
        for z in range(planes):
            halves = []
            for k in range(2):
                total = jnp.zeros((own // 2, 2 * width), F32)
                for s in range(seq):
                    part = got_ref[s * planes + z, :, 2 * k * width : 2 * (k + 1) * width]
                    total += part.astype(F32) * scales[k][s, z]
                halves.append(total)
            both = jnp.concatenate(halves, axis=0).astype(BF16)
            pieces += [both[:, :width], both[:, width:]]
        rows = lax.broadcasted_iota(jnp.int32, (own, hidden_width), 0)
        inner = jnp.zeros((own, hidden_width), F32)
        for i in range(own):
            total = jnp.zeros((own, hidden_width), F32)
            for e in range(expert):
                total += jnp.dot(
                    pieces[e],
                    w_in_ref[i, e * width : (e + 1) * width, :],
                    preferred_element_type=F32,
                )
            inner = jnp.where(rows == i, total, inner)
        hidden = 0.5 * inner * (1.0 + lax.erf(inner * (0.5**0.5)))
        hidden = hidden.astype(BF16)
        hidden_ref[...] = hidden
        core = lax.axis_index("core")
        give_ref[...] = projected(hidden, w_out_ref, 1 - core, planes, width)

    whole = pl.BlockSpec(memory_space=pltpu.VMEM)
    return pl.pallas_call(
        kernel,
        out_shape=[
            jax.ShapeDtypeStruct((own, hidden_width), BF16),
            jax.ShapeDtypeStruct((planes, own, width), BF16),
        ],
        in_specs=[whole, whole, whole],
        out_specs=[whole, whole],
        compiler_params=pltpu.CompilerParams(vmem_limit_bytes=LIMIT),
        cost_estimate=pl.CostEstimate(
            flops=4 * own * width * expert * hidden_width * own,
            bytes_accessed=2 * (w_in.size + w_out.size),
            transcendentals=own * hidden_width,
        ),
        name="experts",
    )(
        got,
        pltpu.with_memory_space_constraint(w_in, pltpu.VMEM),
        pltpu.with_memory_space_constraint(w_out, pltpu.VMEM),
    )


def mix(combine, back, seq, planes):
    slots, count = combine.shape
    pair, width = back.shape[1:]
    own = pair // 2
    steps = count // MIX

    def kernel(combine_ref, back_ref, out_ref, held_ref, sems):
        core = lax.axis_index("core")
        parts = []
        for z in range(planes):
            total = jnp.zeros((pair, width), F32)
            for s in range(seq):
                total += back_ref[s * planes + z].astype(F32)
            near, far = total[:own], total[own:]
            parts += [jnp.where(core == 0, near, far), jnp.where(core == 0, far, near)]
        table = jnp.concatenate(parts, axis=0).astype(BF16)
        copies = []
        for step in range(steps):
            rows = pl.ds(step * MIX, MIX)
            held_ref[rows, :] = lax.dot_general(
                combine_ref[:, rows], table, (((0,), (0,)), ((), ())), preferred_element_type=F32
            )
            copy = pltpu.make_async_copy(held_ref.at[rows], out_ref.at[rows], sems.at[step])
            copy.start()
            copies.append(copy)
        for copy in copies:
            copy.wait()

    whole = pl.BlockSpec(memory_space=pltpu.VMEM)
    return pl.pallas_call(
        kernel,
        out_shape=jax.ShapeDtypeStruct((count, width), F32),
        in_specs=[whole, whole],
        out_specs=pl.BlockSpec(memory_space=pltpu.HBM),
        scratch_shapes=[
            pltpu.VMEM((count, width), F32),
            pltpu.SemaphoreType.DMA((steps,)),
        ],
        compiler_params=pltpu.CompilerParams(vmem_limit_bytes=LIMIT),
        cost_estimate=pl.CostEstimate(
            flops=2 * slots * count * width, bytes_accessed=4 * count * width, transcendentals=0
        ),
        name="mix",
    )(combine, back)


def local(tokens, slot_keys, w_in, w_out):
    seq = lax.axis_size("seq")
    planes = lax.axis_size("plane")
    expert = 2 * planes

    theirs, held = scores(tokens, slot_keys)
    theirs, tokens = lax.optimization_barrier((theirs, tokens))
    gained = swap(theirs, "core")
    mine, held = scores(tokens, slot_keys, held)
    gained, mine = lax.optimization_barrier((gained, mine))
    mine, sent = encode(mine, gained)
    sent, w_in, w_out = lax.optimization_barrier((sent, w_in, w_out))
    code = swap(sent, "plane")
    other = swap(mine, "core")
    held = (held, swap(held, "core"))
    w_in, w_out = staged(w_in, w_out)
    code, w_in, w_out = lax.optimization_barrier((code, w_in, w_out))
    codes = (code, swap(code, "core"))
    send, logits = weigh((mine, other), codes, held, seq, planes)
    got = lax.all_to_all(send, ("seq", "plane"), 0, 0)
    hidden, give = experts(got, w_in, w_out, seq, expert)
    taken = swap(give, "core")
    keep, combine = kept(hidden, w_out, logits, planes)
    back = packed(keep, taken, seq)
    back = lax.all_to_all(back, ("seq", "plane"), 0, 0)
    return mix(combine, back, seq, planes)


def solution(mesh):
    clips, seq, expert = mesh.devices.shape
    split = jax.sharding.Mesh(
        mesh.devices.reshape(clips, seq, expert // 2, 2), ("clip", "seq", "plane", "core")
    )
    expert = ("plane", "core")
    return jax.shard_map(
        local,
        mesh=split,
        in_specs=(
            P(("clip", "seq"), expert),
            P(expert, None),
            P(expert, None, "seq"),
            P(expert, "seq", None),
        ),
        out_specs=P(("clip", "seq"), expert),
        check_vma=False,
    )
```
